128 devices in a mesh: lat: 8 (over x, y_lo), lon: 16 (over y_hi, z, core).
Axes of the slice: x: 4, y: 4 (y_hi: 2, y_lo: 2; y = y_hi * 2 + y_lo), z: 4, core: 2. Of those that a mesh axis runs over, the one named last changes fastest.
Arguments:
- pool: bfloat16 [64, 768, 1152], P('lat', 'lon'), may hold values from -6 to 6
- vec_ids: int32 [8], replicated, may hold values from 0 to 7, as said below
- winds: float32 [64, 768, 288], P('lat', 'lon'), may hold values from -0.3 to 0.3
- wind_ids: int32 [4], replicated, may hold values from 0 to 1
- mixing: float32 [142], replicated, may hold values from 0.01 to 0.05
- basis: bfloat16 [64, 768, 1152], P('lat', 'lon'), may hold values from -6 to 6
Outputs:
- sensitivity: float32 [64, 768, 1152], P('lat', 'lon')
- ritz: float32 [1152, 1152], P('lat', 'lon')
The draws below stay inside these ranges and needn't reach their ends.
Inputs may be any that keep to these rules, and one draw needn't show every extreme that they name: `vec_ids`: the entries are distinct and one of them is 7.
All inputs are finite; a program needn't handle non-finite values.
Results may differ from the reference program's by a relative error of at most 0.0029.
Values sent between devices are 32-bit elements; how exact they have to be, the bound alone decides.
No kernel may reach another device: no remote copies, remote signals or barrier semaphores. Data moves between devices by JAX's collectives and lax.ppermute only.
A program may use at most 128 MiB of HBM per device.

```python
import math
import jax
import jax.numpy as jnp
from jax import lax

LAT_DEV = 8
LEV = 72
TR = 2
VEC = 8
POOL = 8
BASIS = 8
NSLAB = 2
STEPS = 4
NLAT = 64
NLON = 768
N_LAT = 8


def draw_vec_ids(key, part):
    first_key, second_key = jax.random.split(jax.random.fold_in(key, 11))
    others = jax.random.permutation(first_key, POOL - 1)[:VEC - 1]
    chosen = jnp.concatenate([others.astype(jnp.int32), jnp.full((1,), POOL - 1, jnp.int32)])
    return jax.random.permutation(second_key, chosen).astype(jnp.int32)


def touch_ends(array, stream_key, low, largest):
    place = [jax.random.randint(jax.random.fold_in(stream_key, axis), (), 0, length) for axis, length in enumerate(array.shape)]
    main_axis = array.shape.index(max(array.shape))
    beside = place[:main_axis] + [(place[main_axis] + 1) % array.shape[main_axis]] + place[main_axis + 1:]
    return array.at[tuple(place)].set(low).at[tuple(beside)].set(largest)


def levels(key, dims, cuts, smallest, high):
    level = 1.0
    for dim, parts in cuts:
        heights = jax.random.uniform(jax.random.fold_in(jax.random.fold_in(key, 6), dim), (parts,), jnp.float32, smallest / len(cuts), high / len(cuts))
        level = level * jnp.repeat(jnp.exp(heights), dims[dim] // parts).reshape((-1,) + (1,) * (len(dims) - 1 - dim))
    return level


def gaussian(stream_key, shape, scale, reach, pieces=(), kind=jnp.bfloat16):
    array = scale * jax.random.normal(stream_key, shape, jnp.float32)
    if pieces:
        array = array * levels(stream_key, shape, pieces, -0.22, 0.18)
    return jnp.clip(array, -reach, reach).astype(kind)


def setup_inputs(seed: int = 0) -> dict:
    arg_keys = jax.random.split(jax.random.key(seed), 7)
    pool = gaussian(arg_keys[0], (NLAT, NLON, POOL * TR * LEV), 1.0, 6.0, ((0, 8), (1, 16)))
    vec_ids = draw_vec_ids(jax.random.fold_in(arg_keys[6], 71), 0)
    winds = jnp.clip(jax.random.uniform(arg_keys[2], (NLAT, NLON, NSLAB * 2 * LEV), jnp.float32, -0.3, 0.3) * levels(arg_keys[2], (NLAT, NLON, NSLAB * 2 * LEV), ((0, 8), (1, 16)), -0.4, 0.0), -0.3, 0.3)
    wind_ids = touch_ends(jax.random.randint(arg_keys[3], (STEPS,), 0, NSLAB), jax.random.fold_in(arg_keys[3], 1), 0, NSLAB - 1).astype(jnp.int32)
    mixing = jnp.clip(jnp.exp(jax.random.uniform(arg_keys[4], (TR * (LEV - 1),), jnp.float32, math.log(0.01), math.log(0.05))), 0.01, 0.05)
    basis = gaussian(arg_keys[5], (NLAT, NLON, BASIS * TR * LEV), 1.0, 6.0, ((0, 8), (1, 16)))
    return dict(pool=pool, vec_ids=vec_ids, winds=winds, wind_ids=wind_ids, mixing=mixing, basis=basis)


DIFFUSE = 0.075

def channel_coefficients(mixing):
    level_mix = mixing.reshape(TR, LEV - 1)
    padded = jnp.concatenate([level_mix, jnp.zeros((TR, 1), mixing.dtype)], axis=1)
    return jnp.tile(padded.reshape(TR * LEV), VEC)

def select_winds(winds, slab_index):
    tile_rows, tile_cols = (winds.shape[0], winds.shape[1])
    layered = winds.reshape(tile_rows, tile_cols, NSLAB, 2, LEV)
    chosen = lax.dynamic_index_in_dim(layered, slab_index, axis=2, keepdims=False)
    wind_east = jnp.tile(chosen[:, :, 0], (1, 1, VEC * TR))
    wind_north = jnp.tile(chosen[:, :, 1], (1, 1, VEC * TR))
    return (wind_east, wind_north)

def update(state_now, north_side, south_side, east_side, west_side, wind_east, wind_north, coefficient):
    advect = jnp.maximum(wind_east, 0.0) * (east_side - state_now) + jnp.maximum(-wind_east, 0.0) * (west_side - state_now) + jnp.maximum(wind_north, 0.0) * (north_side - state_now) + jnp.maximum(-wind_north, 0.0) * (south_side - state_now)
    spread = DIFFUSE * (north_side + south_side + (east_side + west_side) - 4.0 * state_now)
    flux_up = coefficient * (jnp.roll(state_now, -1, axis=-1) - state_now)
    vertical = flux_up - jnp.roll(flux_up, 1, axis=-1)
    return state_now + advect + spread + vertical

def reference(pool, vec_ids, winds, wind_ids, mixing, basis):
    channels = VEC * TR * LEV
    basis_rows = BASIS * TR * LEV
    grouped = pool.reshape(NLAT, NLON, POOL, TR * LEV)
    state_now = jnp.take(grouped, vec_ids, axis=2).reshape(NLAT, NLON, channels).astype(jnp.float32)
    coefficient = channel_coefficients(mixing)
    for step_index in range(STEPS):
        south_pole = jnp.roll(state_now[:1], NLON // 2, axis=1)
        north_pole = jnp.roll(state_now[-1:], NLON // 2, axis=1)
        extended = jnp.concatenate([south_pole, state_now, north_pole], axis=0)
        slab_index = wind_ids[step_index]

        def lat_block(block_id):
            start = (block_id * LAT_DEV).astype(jnp.int32)
            strip = lax.dynamic_slice_in_dim(extended, start, LAT_DEV + 2, 0)
            centre = strip[1:-1]
            wind_strip = lax.dynamic_slice_in_dim(winds, start, LAT_DEV, 0)
            wind_east, wind_north = select_winds(wind_strip, slab_index)
            east_side = jnp.roll(centre, -1, axis=1)
            west_side = jnp.roll(centre, 1, axis=1)
            return update(centre, strip[2:], strip[:-2], east_side, west_side, wind_east, wind_north, coefficient)
        blocks = lax.map(lat_block, jnp.arange(N_LAT, dtype=jnp.int32))
        state_now = blocks.reshape(NLAT, NLON, channels)
    weights = jnp.cos((jnp.arange(NLAT).astype(jnp.float32) + 0.5) * (math.pi / NLAT) - math.pi / 2)

    def gram_block(running, block_id):
        start = (block_id * LAT_DEV).astype(jnp.int32)
        strip_part = lax.dynamic_slice_in_dim(state_now, start, LAT_DEV, 0)
        strip_weights = lax.dynamic_slice_in_dim(weights, start, LAT_DEV, 0)
        weighted = (strip_weights[:, None, None] * strip_part).astype(jnp.bfloat16).reshape(LAT_DEV * NLON, channels)
        picked = lax.dynamic_slice_in_dim(basis, start, LAT_DEV, 0).reshape(LAT_DEV * NLON, basis_rows)
        return (running + jnp.dot(picked.T, weighted, preferred_element_type=jnp.float32), None)
    running, unused = lax.scan(gram_block, jnp.zeros((basis_rows, channels), jnp.float32), jnp.arange(N_LAT, dtype=jnp.int32))
    ritz = running * (1.0 / math.sqrt(NLAT * NLON))
    return (state_now, ritz)
```

```python
import functools
import math

import jax
import jax.numpy as jnp
import numpy as np
from jax import lax
from jax.experimental import pallas as pl
from jax.experimental.pallas import tpu as pltpu
from jax.sharding import PartitionSpec as P

LEV = 72
TR = 2
VEC = 8
POOL = 8
NSLAB = 2
STEPS = 4
DIFFUSE = 0.075
ALL = ("lat", "lon")

ROWS = 8
COLS = 48
CH = VEC * TR * LEV
GROUP = TR * LEV
WCH = NSLAB * 2 * LEV
D = STEPS
EXT = ROWS + 2 * D
PITCH = 80
FIRST = 16
SPAN = 64
WPACK = 896
BLOCK = 88


def place(x, y, z, core):
    return (x * 2 + y % 2) * 16 + (y // 2) * 8 + z * 2 + core


PLACES = [(x, y, z, c) for x in range(4) for y in range(4) for z in range(4) for c in range(2)]


def moved(dx=0, dy=0, dz=0, dc=0):
    return [
        (place(x, y, z, c), place((x + dx) % 4, (y + dy) % 4, (z + dz) % 4, c ^ dc))
        for x, y, z, c in PLACES
    ]


def meridian():
    pairs = []
    for b in range(8):
        for a in range(8):
            pairs.append((a * 16 + b, (a + 1) * 16 + b if a < 7 else a * 16 + b + 8))
            pairs.append((a * 16 + b + 8, (a - 1) * 16 + b + 8 if a > 0 else a * 16 + b))
    return pairs


FORWARD = meridian()
OVER = [(b, b + 8) for b in range(8)] + [(7 * 16 + b + 8, 7 * 16 + b) for b in range(8)]
BACKWARD = [(t, s) for s, t in FORWARD if (t, s) not in OVER]
OVER_FIRST = [(b, 16 + b + 8) for b in range(8)] + [(7 * 16 + b + 8, 6 * 16 + b) for b in range(8)]
OVER_SECOND = [(16 + b + 8, b + 8) for b in range(8)] + [(6 * 16 + b, 7 * 16 + b) for b in range(8)]
EASTWARD = [(b, (b + 1) % 16) for b in range(16)]
WESTWARD = [(t, s) for s, t in EASTWARD]


def along_meridian(to_next, to_last):
    before = lax.ppermute(to_next, ALL, FORWARD)
    over = lax.ppermute(to_last, ALL, OVER_FIRST)
    after = lax.ppermute(to_last, ALL, BACKWARD)
    return before, after, lax.ppermute(over, ALL, OVER_SECOND)


def pack_kernel(info, vec_ids, pool, winds, low, high, wind, to_next, to_last, chosen):
    lane = lax.broadcasted_iota(jnp.int32, (1, CH), 1)
    source = lane
    for k in range(VEC):
        inside = (lane >= k * GROUP) & (lane < (k + 1) * GROUP)
        source = jnp.where(inside, lane + (vec_ids[k] - k) * GROUP, source)
    for i in range(CH // 128):
        row = lax.broadcasted_iota(jnp.int32, (128, CH), 0) + i * 128
        chosen[i * 128 : (i + 1) * 128, :] = jnp.where(row == source, 1.0, 0.0).astype(jnp.bfloat16)
    for half in range(2):
        rows = pool[half * 4 : half * 4 + 4].reshape(4 * COLS, CH)
        picked = jnp.dot(rows, chosen[...], preferred_element_type=jnp.float32)
        picked = picked.reshape(4, COLS, CH)

        @pl.when(info[0] == 0)
        def _():
            (low, high)[half][...] = picked

        @pl.when(info[0] != 0)
        def _():
            for r in range(4):
                (high, low)[half][3 - r] = picked[r]

    place_in_slab = lax.rem(lax.broadcasted_iota(jnp.int32, (1, WCH), 1), 2 * LEV)
    turn = jnp.where((place_in_slab >= LEV) & (info[0] != 0), -1.0, 1.0)
    for r in range(ROWS):
        own = jnp.where(info[0] == 0, r, ROWS - 1 - r)
        line = winds[own] * turn
        wind[r] = line
        if r < 3:
            to_last[:, r * WCH : (r + 1) * WCH] = line
        if r >= ROWS - 3:
            to_next[:, (r - ROWS + 3) * WCH : (r - ROWS + 4) * WCH] = line


def pack(info, vec_ids, pool, winds):
    shapes = [(4, COLS, CH), (4, COLS, CH), (ROWS, COLS, WCH), (COLS, WPACK), (COLS, WPACK)]
    return pl.pallas_call(
        pack_kernel,
        out_shape=[jax.ShapeDtypeStruct(s, jnp.float32) for s in shapes],
        in_specs=[pl.BlockSpec(memory_space=pltpu.SMEM)] * 2
        + [pl.BlockSpec(memory_space=pltpu.VMEM)] * 2,
        out_specs=[pl.BlockSpec(memory_space=pltpu.VMEM)] * 5,
        scratch_shapes=[pltpu.VMEM((CH, CH), jnp.bfloat16)],
        compiler_params=pltpu.CompilerParams(vmem_limit_bytes=40 << 20),
        cost_estimate=pl.CostEstimate(flops=1 << 30, bytes_accessed=4 << 20, transcendentals=0),
        name="pack",
    )(info, vec_ids, pool, winds)


def main_kernel(
    info, wind_ids, cosine, south, low, high, north, over, west, east,
    wind_south, wind, wind_north, wind_over, wind_west, wind_east,
    levels, mix, basis_main, basis_rest,
    out, mine, theirs,
    state_a, state_b, wind_ext, spread, weighted, gram, rest,
):
    flip, mx, my, mz, mc, is_over, turn_west, turn_east = (info[i] for i in range(8))
    inner = slice(FIRST, FIRST + COLS)

    for r in range(4):
        state_a[r, inner] = south[r]
        state_a[4 + r, inner] = low[r]
        state_a[8 + r, inner] = high[r]

    @pl.when(is_over == 0)
    def _():
        for r in range(4):
            state_a[12 + r, inner] = north[r]

    @pl.when(is_over != 0)
    def _():
        for r in range(4):
            state_a[12 + r, inner] = over[r]

    for r in range(EXT):
        from_west = jnp.where(turn_west == 0, r, EXT - 1 - r)
        from_east = jnp.where(turn_east == 0, r, EXT - 1 - r)
        state_a[r, FIRST - 4 : FIRST] = west[from_west]
        state_a[r, FIRST + COLS : FIRST + COLS + 4] = east[from_east]

    for r in range(3):
        lanes = slice(r * WCH, (r + 1) * WCH)
        wind_ext[r, 8 : 8 + COLS] = wind_south[:, lanes]
        after = jnp.where(is_over == 0, wind_north[:, lanes], wind_over[:, lanes])
        wind_ext[11 + r, 8 : 8 + COLS] = after
    for r in range(ROWS):
        wind_ext[3 + r, 8 : 8 + COLS] = wind[r]
    lane = lax.rem(lax.broadcasted_iota(jnp.int32, (1, WCH), 1), 2 * LEV)
    for r in range(EXT - 2):
        from_west = jnp.where(turn_west == 0, r, EXT - 3 - r)
        from_east = jnp.where(turn_east == 0, r, EXT - 3 - r)
        sign_west = jnp.where((lane >= LEV) & (turn_west != 0), -1.0, 1.0)
        sign_east = jnp.where((lane >= LEV) & (turn_east != 0), -1.0, 1.0)
        wind_ext[r, 4:8] = wind_west[from_west] * sign_west
        wind_ext[r, 8 + COLS : 12 + COLS] = wind_east[from_east] * sign_east

    level = lax.broadcasted_iota(jnp.int32, (2 * LEV, CH), 0)
    level = jnp.where(level >= LEV, level - LEV, level)
    repeat = jnp.where(level == levels[...], 1.0, 0.0).astype(jnp.bfloat16)
    flat = wind_ext[...].reshape((EXT - 2) * SPAN, WCH)
    for i in range(2 * NSLAB):
        value = flat[:, i * LEV : (i + 1) * LEV]
        coarse = value.astype(jnp.bfloat16)
        fine = (value - coarse.astype(jnp.float32)).astype(jnp.bfloat16)
        both = jnp.concatenate([coarse, fine], axis=1)
        spread[i] = jnp.dot(both, repeat, preferred_element_type=jnp.float32).reshape(
            EXT - 2, SPAN, CH
        )

    up, down = mix[0:1, :], mix[1:2, :]

    def updated(source, slab, r, c):
        now = source[r, pl.ds(c, 8), :]
        after = source[r + 1, pl.ds(c, 8), :]
        before = source[r - 1, pl.ds(c, 8), :]
        east_side = source[r, pl.ds(c + 1, 8), :]
        west_side = source[r, pl.ds(c - 1, 8), :]
        u = spread[2 * slab, r - 1, pl.ds(c - FIRST + 8, 8), :]
        v = spread[2 * slab + 1, r - 1, pl.ds(c - FIRST + 8, 8), :]
        gain_east = jnp.maximum(u, 0.0) + DIFFUSE
        gain_after = jnp.maximum(v, 0.0) + DIFFUSE
        change = gain_east * (east_side - now) + (gain_east - u) * (west_side - now)
        change += gain_after * (after - now) + (gain_after - v) * (before - now)
        change += up * (pltpu.roll(now, CH - 1, 1) - now) - down * (now - pltpu.roll(now, 1, 1))
        return now + change

    buffers = (state_a, state_b)
    for step in range(STEPS - 1):
        source, target = buffers[step % 2], buffers[(step + 1) % 2]
        slab = wind_ids[step]

        def body(r, carry):
            for c in range(FIRST - 8, FIRST - 8 + SPAN, 8):
                target[r, c : c + 8, :] = updated(source, slab, r, c)
            return carry

        lax.fori_loop(1 + step, EXT - 1 - step, body, 0)

    source = buffers[(STEPS - 1) % 2]
    slab = wind_ids[STEPS - 1]

    def last(r, carry):
        own = jnp.where(flip == 0, r - D, ROWS - 1 - (r - D))
        share = cosine[own]
        for c in range(0, COLS, 16):
            first = updated(source, slab, r, FIRST + c)
            second = updated(source, slab, r, FIRST + c + 8)
            out[own, c : c + 8, :] = first
            out[own, c + 8 : c + 16, :] = second
            both = jnp.concatenate([first, second], axis=0) * share
            weighted[own, c : c + 16, :] = both.astype(jnp.bfloat16)
        return carry

    lax.fori_loop(D, D + ROWS, last, 0)

    flat_weighted = weighted[...].reshape(ROWS * COLS, CH)
    across = (((0,), (0,)), ((), ()))
    for i in range(CH // 128):
        gram[i * 128 : (i + 1) * 128, :] = lax.dot_general(
            flat_weighted[:, i * 128 : (i + 1) * 128],
            basis_main[...],
            across,
            preferred_element_type=jnp.float32,
        )
    tail = lax.dot_general(
        basis_rest[...], flat_weighted, across, preferred_element_type=jnp.float32
    )
    for g in range(VEC * TR):
        rest[g, :, :LEV] = tail[:, g * LEV : (g + 1) * LEV]

    def place_blocks(i, carry):
        rz, rx, ry = i // 16, (i // 4) % 4, i % 4
        z, x, y = (mz + rz) % 4, (mx + rx) % 4, (my + ry) % 4
        at_first = (rz * 2 + rx // 2) * 4 + (rx % 2) * 2 + ry % 2
        at_second = (rx * 2 + rz // 2) * 4 + (rz % 2) * 2 + ry % 2
        at = jnp.where(ry < 2, at_first, at_second)
        a = x * 2 + y % 2
        for dc, target in ((0, mine), (1, theirs)):
            g = (y // 2) * 8 + z * 2 + (mc ^ dc)
            target[ry // 2, at, :LEV] = gram[
                pl.ds(pl.multiple_of(g * LEV, 8), LEV), pl.ds(pl.multiple_of(a * 128, 128), 128)
            ]
            target[ry // 2, at, LEV:] = rest[g, pl.ds(pl.multiple_of(a * 16, 16), 16), :]
        return carry

    lax.fori_loop(0, 64, place_blocks, 0)


def main(scalars, arrays):
    blocks = jax.ShapeDtypeStruct((2, 32, BLOCK, 128), jnp.float32)
    vmem = pl.BlockSpec(memory_space=pltpu.VMEM)
    return pl.pallas_call(
        main_kernel,
        out_shape=[jax.ShapeDtypeStruct((ROWS, COLS, CH), jnp.float32), blocks, blocks],
        in_specs=[pl.BlockSpec(memory_space=pltpu.SMEM)] * len(scalars) + [vmem] * len(arrays),
        out_specs=[vmem] * 3,
        scratch_shapes=[
            pltpu.VMEM((EXT, PITCH, CH), jnp.float32),
            pltpu.VMEM((EXT, PITCH, CH), jnp.float32),
            pltpu.VMEM((EXT - 2, SPAN, WCH), jnp.float32),
            pltpu.VMEM((2 * NSLAB, EXT - 2, SPAN, CH), jnp.float32),
            pltpu.VMEM((ROWS, COLS, CH), jnp.bfloat16),
            pltpu.VMEM((CH, 1024), jnp.float32),
            pltpu.VMEM((VEC * TR, 128, 128), jnp.float32),
        ],
        compiler_params=pltpu.CompilerParams(vmem_limit_bytes=60 << 20),
        cost_estimate=pl.CostEstimate(flops=4 << 30, bytes_accessed=16 << 20, transcendentals=0),
        name="window",
    )(*scalars, *arrays)


def ring_sum(parts, up, down):
    from_below = lax.ppermute(parts[3:5], ALL, up)
    from_above = lax.ppermute(parts[5:7], ALL, down)
    last_below = lax.ppermute(parts[2] + from_below[1], ALL, up)
    last_above = lax.ppermute(parts[7] + from_above[0], ALL, down)
    return jnp.stack(
        [parts[0] + from_above[1] + last_below, parts[1] + from_below[0] + last_above]
    )


def shards(pool, vec_ids, winds, wind_ids, mixing, basis):
    lat_index = lax.axis_index("lat").astype(jnp.int32)
    lon_index = lax.axis_index("lon").astype(jnp.int32)
    flip = lon_index // 8
    is_over = ((lat_index == 0) & (flip == 1)) | ((lat_index == 7) & (flip == 0))
    info = jnp.stack(
        [
            flip,
            lat_index // 2,
            flip * 2 + lat_index % 2,
            (lon_index // 2) % 4,
            lon_index % 2,
            is_over.astype(jnp.int32),
            (lon_index % 8 == 0).astype(jnp.int32),
            (lon_index % 8 == 7).astype(jnp.int32),
        ]
    )
    low, high, wind, wind_up, wind_down = pack(info, vec_ids, pool, winds)

    wind_south, wind_north, wind_over = along_meridian(wind_up, wind_down)
    south, north, over = along_meridian(high, low)

    crossed = info[5] != 0
    wind_after = jnp.where(crossed, wind_over, wind_north)

    def wind_edge(columns):
        count = 4
        before = wind_south[columns, : 3 * WCH].reshape(count, 3, WCH).transpose(1, 0, 2)
        after = wind_after[columns, : 3 * WCH].reshape(count, 3, WCH).transpose(1, 0, 2)
        return jnp.concatenate([before, wind[:, columns], after], axis=0)

    wind_west = lax.ppermute(wind_edge(slice(COLS - 4, COLS)), "lon", EASTWARD)
    wind_east = lax.ppermute(wind_edge(slice(0, 4)), "lon", WESTWARD)

    def edge(columns):
        after = jnp.where(crossed, over[:, columns], north[:, columns])
        return jnp.concatenate([south[:, columns], low[:, columns], high[:, columns], after], axis=0)

    west = lax.ppermute(edge(slice(COLS - 4, COLS)), "lon", EASTWARD)
    east = lax.ppermute(edge(slice(0, 4)), "lon", WESTWARD)

    level_mix = jnp.concatenate(
        [mixing.reshape(TR, LEV - 1), jnp.zeros((TR, 1), mixing.dtype)], axis=1
    )
    upper = jnp.tile(level_mix.reshape(GROUP), VEC)
    mix = jnp.stack([upper, jnp.roll(upper, 1)])
    levels = jnp.asarray(np.arange(CH, dtype=np.int32)[None] % LEV)
    rows = (jnp.arange(ROWS, dtype=jnp.int32) + lat_index * ROWS).astype(jnp.float32)
    cosine = jnp.cos((rows + 0.5) * (math.pi / (ROWS * 8)) - math.pi / 2)
    grouped = basis.reshape(ROWS * COLS, 8, 144)
    basis_main = grouped[:, :, :128].reshape(ROWS * COLS, 1024)
    basis_rest = grouped[:, :, 128:].reshape(ROWS * COLS, 128)

    sensitivity, mine, theirs = main(
        (info, wind_ids, cosine),
        (
            south, low, high, north, over, west, east,
            wind_south, wind, wind_north, wind_over, wind_west, wind_east,
            levels, mix, basis_main, basis_rest,
        ),
    )

    total = mine + lax.ppermute(theirs, ALL, moved(dc=1))
    z_up, z_down, x_up, x_down = moved(dz=1), moved(dz=-1), moved(dx=1), moved(dx=-1)
    first = ring_sum(total[0].reshape(8, 4, BLOCK, 128), z_up, z_down)
    second = ring_sum(total[1].reshape(8, 4, BLOCK, 128), x_up, x_down)
    first = ring_sum(first.reshape(8, BLOCK, 128), x_up, x_down)
    second = ring_sum(second.reshape(8, BLOCK, 128), z_up, z_down)
    block = first[0] + lax.ppermute(first[1], ALL, moved(dy=1))
    block += lax.ppermute(second[0], ALL, moved(dy=2)) + lax.ppermute(second[1], ALL, moved(dy=3))
    ritz = jnp.concatenate([block[:LEV].T, block[LEV:, :LEV]], axis=0)
    return sensitivity, ritz * (1.0 / math.sqrt(ROWS * COLS * 128))


def solution(mesh):
    in_specs = (P("lat", "lon", None), P(), P("lat", "lon", None), P(), P(), P("lat", "lon", None))
    out_specs = (P("lat", "lon", None), P("lat", "lon"))
    return jax.shard_map(shards, mesh=mesh, in_specs=in_specs, out_specs=out_specs, check_vma=False)
```

```python
import functools
import functools
import math

import jax
import jax.numpy as jnp
import numpy as np
from jax import lax
from jax.experimental import pallas as pl
from jax.experimental.pallas import tpu as pltpu
from jax.sharding import PartitionSpec as P

LEV = 72
TR = 2
VEC = 8
POOL = 8
NSLAB = 2
STEPS = 4
DIFFUSE = 0.075
ALL = ("lat", "lon")

ROWS = 8
COLS = 48
CH = VEC * TR * LEV
GROUP = TR * LEV
WCH = NSLAB * 2 * LEV
D = STEPS
EXT = ROWS + 2 * D
PITCH = 80
FIRST = 16
SPAN = 64
WPACK = 896
PART = 640
BLOCK = 88


def place(x, y, z, core):
    return (x * 2 + y % 2) * 16 + (y // 2) * 8 + z * 2 + core


PLACES = [(x, y, z, c) for x in range(4) for y in range(4) for z in range(4) for c in range(2)]


def moved(dx=0, dy=0, dz=0, dc=0):
    return [
        (place(x, y, z, c), place((x + dx) % 4, (y + dy) % 4, (z + dz) % 4, c ^ dc))
        for x, y, z, c in PLACES
    ]


def turned(bits):
    return [(place(x, y, z, c), place(x, y ^ bits, z, c)) for x, y, z, c in PLACES]


def meridian():
    pairs = []
    for b in range(8):
        for a in range(8):
            pairs.append((a * 16 + b, (a + 1) * 16 + b if a < 7 else a * 16 + b + 8))
            pairs.append((a * 16 + b + 8, (a - 1) * 16 + b + 8 if a > 0 else a * 16 + b))
    return pairs


FORWARD = meridian()
BACKWARD = [(t, s) for s, t in FORWARD]
EASTWARD = [(b, (b + 1) % 16) for b in range(16)]
WESTWARD = [(t, s) for s, t in EASTWARD]


def edge_tile(r, m):
    i = r * (CH // 128) + m
    return slice(i // 6 * 8, i // 6 * 8 + 8), slice(WPACK + i % 6 * 128, WPACK + i % 6 * 128 + 128)


def pack_kernel(
    info, vec_ids, pool, winds, low, high, wind, edge_next, edge_last,
    next_0, next_1, last_0, last_1, chosen,
):
    lane = lax.broadcasted_iota(jnp.int32, (1, CH), 1)
    source = lane
    for k in range(VEC):
        inside = (lane >= k * GROUP) & (lane < (k + 1) * GROUP)
        source = jnp.where(inside, lane + (vec_ids[k] - k) * GROUP, source)
    for i in range(CH // 128):
        row = lax.broadcasted_iota(jnp.int32, (128, CH), 0) + i * 128
        chosen[i * 128 : (i + 1) * 128, :] = jnp.where(row == source, 1.0, 0.0).astype(jnp.bfloat16)
    for half in range(2):
        rows = pool[half * 4 : half * 4 + 4].reshape(4 * COLS, CH)
        picked = jnp.dot(rows, chosen[...], preferred_element_type=jnp.float32)
        picked = picked.reshape(4, COLS, CH)

        @pl.when(info[0] == 0)
        def _():
            (low, high)[half][...] = picked

        @pl.when(info[0] != 0)
        def _():
            for r in range(4):
                (high, low)[half][3 - r] = picked[r]

    place_in_slab = lax.rem(lax.broadcasted_iota(jnp.int32, (1, WCH), 1), 2 * LEV)
    turn = jnp.where((place_in_slab >= LEV) & (info[0] != 0), -1.0, 1.0)
    for r in range(ROWS):
        own = jnp.where(info[0] == 0, r, ROWS - 1 - r)
        line = winds[own] * turn
        wind[r] = line
        if r < 3:
            edge_last[:, r * WCH : (r + 1) * WCH] = line
        if r >= ROWS - 3:
            edge_next[:, (r - ROWS + 3) * WCH : (r - ROWS + 4) * WCH] = line
    for rows, edge, bulk_0, bulk_1 in (
        (high, edge_next, next_0, next_1),
        (low, edge_last, last_0, last_1),
    ):
        for r in range(4):
            for m in range(CH // 128):
                lanes = slice(m * 128, (m + 1) * 128)
                ends = jnp.concatenate([rows[r, :4, lanes], rows[r, COLS - 4 :, lanes]], axis=0)
                where = edge_tile(r, m)
                edge[where[0], where[1]] = ends
            bulk_0[r] = rows[r, 4 : COLS - 4, :PART]
            bulk_1[r] = rows[r, 4 : COLS - 4, PART:]


def pack(info, vec_ids, pool, winds):
    shapes = [(4, COLS, CH)] * 2 + [(ROWS, COLS, WCH)] + [(COLS, WPACK + 768)] * 2
    shapes += [(4, COLS - 8, PART), (4, COLS - 8, CH - PART)] * 2
    return pl.pallas_call(
        pack_kernel,
        out_shape=[jax.ShapeDtypeStruct(s, jnp.float32) for s in shapes],
        in_specs=[pl.BlockSpec(memory_space=pltpu.SMEM)] * 2
        + [pl.BlockSpec(memory_space=pltpu.VMEM)] * 2,
        out_specs=[pl.BlockSpec(memory_space=pltpu.VMEM)] * 9,
        scratch_shapes=[pltpu.VMEM((CH, CH), jnp.bfloat16)],
        compiler_params=pltpu.CompilerParams(vmem_limit_bytes=24 << 20),
        cost_estimate=pl.CostEstimate(flops=1 << 30, bytes_accessed=4 << 20, transcendentals=0),
        name="pack",
    )(info, vec_ids, pool, winds)


SIDE = EXT - 2


def edges_kernel(before, after, low, high, wind, *rest):
    to_east, to_west = rest[4:6]
    for first, near, target in ((COLS - 4, 4, to_east), (0, 0, to_west)):
        columns = slice(first, first + 4)
        for r in range(3):
            for m in range(CH // 128):
                lanes = slice(m * 128, (m + 1) * 128)
                where = edge_tile(r + 1, m)
                target[r, :, lanes] = before[where[0], where[1]][near : near + 4]
                where = edge_tile(r, m)
                target[11 + r, :, lanes] = after[where[0], where[1]][near : near + 4]
        for r in range(4):
            target[3 + r] = low[r, columns, :]
            target[7 + r] = high[r, columns, :]
        for r in range(SIDE):
            if r < 3:
                line = before[columns, r * WCH : (r + 1) * WCH]
            elif r < 11:
                line = wind[r - 3, columns, :]
            else:
                line = after[columns, (r - 11) * WCH : (r - 10) * WCH]
            target[SIDE + r // 4, :, r % 4 * WCH : (r % 4 + 1) * WCH] = line


def edges(arrays, bulk):
    vmem = pl.BlockSpec(memory_space=pltpu.VMEM)
    anywhere = pl.BlockSpec(memory_space=pl.ANY)
    shapes = [jax.ShapeDtypeStruct((SIDE + 4, 4, CH), jnp.float32)] * 2
    return pl.pallas_call(
        edges_kernel,
        out_shape=shapes + [jax.ShapeDtypeStruct(b.shape, b.dtype) for b in bulk],
        in_specs=[vmem] * 5 + [anywhere] * 4,
        out_specs=[vmem] * 2 + [anywhere] * 4,
        input_output_aliases={5 + i: 2 + i for i in range(4)},
        compiler_params=pltpu.CompilerParams(vmem_limit_bytes=16 << 20),
        cost_estimate=pl.CostEstimate(flops=1 << 20, bytes_accessed=4 << 20, transcendentals=0),
        name="edges",
    )(*arrays, *bulk)


def frame_kernel(info, before, after, wind, west, east, wind_ext):
    turn_west, turn_east = info[5], info[6]
    for r in range(3):
        lanes = slice(r * WCH, (r + 1) * WCH)
        wind_ext[r, 8 : 8 + COLS] = before[:, lanes]
        wind_ext[11 + r, 8 : 8 + COLS] = after[:, lanes]
    for r in range(ROWS):
        wind_ext[3 + r, 8 : 8 + COLS] = wind[r]
    lane = lax.rem(lax.broadcasted_iota(jnp.int32, (1, WCH), 1), 2 * LEV)
    for turn, payload, first in ((turn_west, west, 4), (turn_east, east, 8 + COLS)):
        sign = jnp.where((lane >= LEV) & (turn != 0), -1.0, 1.0)
        for r in range(SIDE):
            line = payload[SIDE + r // 4, :, r % 4 * WCH : (r % 4 + 1) * WCH] * sign
            wind_ext[jnp.where(turn == 0, r, SIDE - 1 - r), first : first + 4] = line


def frame_winds(info, *arrays):
    vmem = pl.BlockSpec(memory_space=pltpu.VMEM)
    return pl.pallas_call(
        frame_kernel,
        out_shape=jax.ShapeDtypeStruct((SIDE, SPAN, WCH), jnp.float32),
        in_specs=[pl.BlockSpec(memory_space=pltpu.SMEM)] + [vmem] * 5,
        out_specs=vmem,
        compiler_params=pltpu.CompilerParams(vmem_limit_bytes=16 << 20),
        cost_estimate=pl.CostEstimate(flops=1 << 20, bytes_accessed=4 << 20, transcendentals=0),
        name="frame",
    )(info, *arrays)


def window_kernel(
    part, info, wind_ids, cosine,
    before_edge, low, high, after_edge, west, east, wind_ext,
    levels, mix, basis_main, basis_rest, before_0, after_0,
    *others,
):
    before_1, after_1, earlier = others[:3] if part else (None, None, None)
    out, mine, theirs, state_a, state_b, spread, weighted, gram, rest = others[3 * part :]
    flip, mx, my, mz, mc, turn_west, turn_east = (info[i] for i in range(7))
    lanes = slice(part * 512, part * 512 + PART)
    skip = part * 64

    for r in range(4):
        state_a[4 + r, FIRST : FIRST + COLS] = low[r, :, lanes]
        state_a[8 + r, FIRST : FIRST + COLS] = high[r, :, lanes]
        for row, edge, bulk_0, bulk_1 in (
            (r, before_edge, before_0, before_1),
            (12 + r, after_edge, after_0, after_1),
        ):
            middle = slice(FIRST + 4, FIRST + COLS - 4)
            if part:
                state_a[row, middle, :128] = bulk_0[r, :, 512:]
                state_a[row, middle, 128:] = bulk_1[r]
            else:
                state_a[row, middle] = bulk_0[r]
            for m in range(PART // 128):
                tile = slice(m * 128, (m + 1) * 128)
                where = edge_tile(r, m + part * 4)
                ends = edge[where[0], where[1]]
                state_a[row, FIRST : FIRST + 4, tile] = ends[:4]
                state_a[row, FIRST + COLS - 4 : FIRST + COLS, tile] = ends[4:]
    for r in range(SIDE):
        from_west = jnp.where(turn_west == 0, r, SIDE - 1 - r)
        from_east = jnp.where(turn_east == 0, r, SIDE - 1 - r)
        state_a[1 + r, FIRST - 4 : FIRST] = west[from_west, :, lanes]
        state_a[1 + r, FIRST + COLS : FIRST + COLS + 4] = east[from_east, :, lanes]

    level = lax.broadcasted_iota(jnp.int32, (2 * LEV, PART), 0)
    level = jnp.where(level >= LEV, level - LEV, level)
    repeat = jnp.where(level == levels[:, lanes], 1.0, 0.0).astype(jnp.bfloat16)
    flat = wind_ext[...].reshape(SIDE * SPAN, WCH)
    for i in range(2 * NSLAB):
        value = flat[:, i * LEV : (i + 1) * LEV]
        coarse = value.astype(jnp.bfloat16)
        fine = (value - coarse.astype(jnp.float32)).astype(jnp.bfloat16)
        both = jnp.concatenate([coarse, fine], axis=1)
        spread[i] = jnp.dot(both, repeat, preferred_element_type=jnp.float32).reshape(
            SIDE, SPAN, PART
        )

    up, down = mix[0:1, lanes], mix[1:2, lanes]

    def updated(source, slab, r, c):
        now = source[r, pl.ds(c, 8), :]
        after = source[r + 1, pl.ds(c, 8), :]
        before = source[r - 1, pl.ds(c, 8), :]
        east_side = source[r, pl.ds(c + 1, 8), :]
        west_side = source[r, pl.ds(c - 1, 8), :]
        u = spread[2 * slab, r - 1, pl.ds(c - FIRST + 8, 8), :]
        v = spread[2 * slab + 1, r - 1, pl.ds(c - FIRST + 8, 8), :]
        gain_east = jnp.maximum(u, 0.0) + DIFFUSE
        gain_after = jnp.maximum(v, 0.0) + DIFFUSE
        change = gain_east * (east_side - now) + (gain_east - u) * (west_side - now)
        change += gain_after * (after - now) + (gain_after - v) * (before - now)
        above, below = pltpu.roll(now, PART - 1, 1), pltpu.roll(now, 1, 1)
        change += up * (above - now) - down * (now - below)
        return now + change

    buffers = (state_a, state_b)
    for step in range(STEPS - 1):
        source, target = buffers[step % 2], buffers[(step + 1) % 2]
        slab = wind_ids[step]

        def body(r, carry):
            for c in range(FIRST - 8, FIRST - 8 + SPAN, 8):
                target[r, c : c + 8, :] = updated(source, slab, r, c)
            return carry

        lax.fori_loop(1 + step, EXT - 1 - step, body, 0)

    source = buffers[(STEPS - 1) % 2]
    slab = wind_ids[STEPS - 1]
    own_lanes = lax.broadcasted_iota(jnp.int32, (16, 128), 1) >= skip

    def last(r, carry):
        own = jnp.where(flip == 0, r - D, ROWS - 1 - (r - D))
        share = cosine[own]
        for c in range(0, COLS, 16):
            first = updated(source, slab, r, FIRST + c)
            second = updated(source, slab, r, FIRST + c + 8)
            both = jnp.concatenate([first, second], axis=0)
            if part:
                there = slice(c, c + 16)
                out[own, there, :512] = earlier[own, there, :512]
                out[own, there, 512:640] = jnp.where(
                    own_lanes, both[:, :128], earlier[own, there, 512:]
                )
                out[own, there, 640:] = both[:, 128:]
            else:
                out[own, c : c + 16, :] = both
            weighted[own, c : c + 16, :] = (both * share).astype(jnp.bfloat16)
        return carry

    lax.fori_loop(D, D + ROWS, last, 0)

    flat_weighted = weighted[...].reshape(ROWS * COLS, PART)
    across = (((0,), (0,)), ((), ()))
    for i in range(PART // 128):
        gram[i * 128 : (i + 1) * 128, :] = lax.dot_general(
            flat_weighted[:, i * 128 : (i + 1) * 128],
            basis_main[...],
            across,
            preferred_element_type=jnp.float32,
        )
    tail = lax.dot_general(
        basis_rest[...], flat_weighted, across, preferred_element_type=jnp.float32
    )
    for g in range(8):
        rest[g, :, :LEV] = tail[:, skip + g * LEV : skip + (g + 1) * LEV]

    def place_blocks(i, carry):
        rz, rx, ry = i // 8, (i // 2) % 4, i % 2
        z, x = (mz + rz) % 4, (mx + rx) % 4
        outer, inner = (rx, rz) if part else (rz, rx)
        at = outer * 8 + inner * 2 + ry
        a = x * 2 + (my ^ ry)
        for dc, target in ((0, mine), (1, theirs)):
            g = z * 2 + (mc ^ dc)
            target[at, :LEV] = gram[
                pl.ds(pl.multiple_of(skip + g * LEV, 8), LEV),
                pl.ds(pl.multiple_of(a * 128, 128), 128),
            ]
            target[at, LEV:] = rest[g, pl.ds(pl.multiple_of(a * 16, 16), 16), :]
        return carry

    lax.fori_loop(0, 32, place_blocks, 0, unroll=4)


def window(part, scalars, arrays):
    blocks = jax.ShapeDtypeStruct((32, BLOCK, 128), jnp.float32)
    vmem = pl.BlockSpec(memory_space=pltpu.VMEM)
    return pl.pallas_call(
        functools.partial(window_kernel, part),
        out_shape=[
            jax.ShapeDtypeStruct((ROWS, COLS, CH if part else PART), jnp.float32),
            blocks,
            blocks,
        ],
        in_specs=[pl.BlockSpec(memory_space=pltpu.SMEM)] * len(scalars) + [vmem] * len(arrays),
        out_specs=[vmem] * 3,
        scratch_shapes=[
            pltpu.VMEM((EXT, PITCH, PART), jnp.float32),
            pltpu.VMEM((EXT, PITCH, PART), jnp.float32),
            pltpu.VMEM((2 * NSLAB, SIDE, SPAN, PART), jnp.float32),
            pltpu.VMEM((ROWS, COLS, PART), jnp.bfloat16),
            pltpu.VMEM((PART, 1024), jnp.float32),
            pltpu.VMEM((8, 128, 128), jnp.float32),
        ],
        compiler_params=pltpu.CompilerParams(vmem_limit_bytes=40 << 20),
        cost_estimate=pl.CostEstimate(flops=8 << 30, bytes_accessed=16 << 20, transcendentals=0),
        name=f"window_{part}",
    )(*scalars, *arrays)


def line_sum(parts, **axis):
    (name,) = axis
    sent = [lax.ppermute(parts[k], ALL, moved(**{name: k})) for k in (1, 2, 3)]
    return (parts[0] + sent[0]) + (sent[1] + sent[2])


def shards(pool, vec_ids, winds, wind_ids, mixing, basis):
    lat_index = lax.axis_index("lat").astype(jnp.int32)
    lon_index = lax.axis_index("lon").astype(jnp.int32)
    flip = lon_index // 8
    info = jnp.stack(
        [
            flip,
            lat_index // 2,
            lat_index % 2,
            (lon_index // 2) % 4,
            lon_index % 2,
            (lon_index % 8 == 0).astype(jnp.int32),
            (lon_index % 8 == 7).astype(jnp.int32),
        ]
    )
    low, high, wind, edge_next, edge_last, *bulk = pack(info, vec_ids, pool, winds)

    before_edge = lax.ppermute(edge_next, ALL, FORWARD)
    after_edge = lax.ppermute(edge_last, ALL, BACKWARD)
    to_east, to_west, *bulk = edges((before_edge, after_edge, low, high, wind), bulk)
    west = lax.ppermute(to_east, "lon", EASTWARD)
    east = lax.ppermute(to_west, "lon", WESTWARD)
    before_0, after_0 = lax.ppermute(bulk[0], ALL, FORWARD), lax.ppermute(bulk[2], ALL, BACKWARD)
    before_1, after_1 = lax.ppermute(bulk[1], ALL, FORWARD), lax.ppermute(bulk[3], ALL, BACKWARD)
    wind_ext = frame_winds(info, before_edge, after_edge, wind, west, east)

    level_mix = jnp.concatenate(
        [mixing.reshape(TR, LEV - 1), jnp.zeros((TR, 1), mixing.dtype)], axis=1
    )
    upper = jnp.tile(level_mix.reshape(GROUP), VEC)
    mix = jnp.stack([upper, jnp.roll(upper, 1)])
    rows = (jnp.arange(ROWS, dtype=jnp.int32) + lat_index * ROWS).astype(jnp.float32)
    cosine = jnp.cos((rows + 0.5) * (math.pi / (ROWS * 8)) - math.pi / 2)
    grouped = basis.reshape(ROWS * COLS, 8, 144)
    basis_main = grouped[:, :, :128].reshape(ROWS * COLS, 1024)
    basis_rest = grouped[:, :, 128:].reshape(ROWS * COLS, 128)

    levels = jnp.asarray(np.arange(CH, dtype=np.int32)[None] % LEV)
    scalars = (info, wind_ids, cosine)
    arrays = (
        before_edge, low, high, after_edge, west, east, wind_ext,
        levels, mix, basis_main, basis_rest, before_0, after_0,
    )
    half, mine, theirs = window(0, scalars, arrays)
    first = mine + lax.ppermute(theirs, ALL, moved(dc=1))
    sensitivity, mine, theirs = window(1, scalars, (*arrays, before_1, after_1, half))
    second = mine + lax.ppermute(theirs, ALL, moved(dc=1))

    first = line_sum(first.reshape(4, 8, BLOCK, 128), dz=1)
    second = line_sum(second.reshape(4, 8, BLOCK, 128), dx=1)
    first = line_sum(first.reshape(4, 2, BLOCK, 128), dx=1)
    second = line_sum(second.reshape(4, 2, BLOCK, 128), dz=1)
    near = jnp.where(flip == 0, first, second)
    far = jnp.where(flip == 0, second, first)
    block = near[0] + lax.ppermute(near[1], ALL, turned(1))
    block += lax.ppermute(far[0], ALL, turned(2)) + lax.ppermute(far[1], ALL, turned(3))
    ritz = jnp.concatenate([block[:LEV].T, block[LEV:, :LEV]], axis=0)
    return sensitivity, ritz * (1.0 / math.sqrt(ROWS * COLS * 128))


def solution(mesh):
    in_specs = (P("lat", "lon", None), P(), P("lat", "lon", None), P(), P(), P("lat", "lon", None))
    out_specs = (P("lat", "lon", None), P("lat", "lon"))
    return jax.shard_map(shards, mesh=mesh, in_specs=in_specs, out_specs=out_specs, check_vma=False)
```

```python
import functools
import functools
import math

import jax
import jax.numpy as jnp
import numpy as np
from jax import lax
from jax.experimental import pallas as pl
from jax.experimental.pallas import tpu as pltpu
from jax.sharding import PartitionSpec as P

LEV = 72
TR = 2
VEC = 8
POOL = 8
NSLAB = 2
STEPS = 4
DIFFUSE = 0.075
ALL = ("lat", "lon")

ROWS = 8
COLS = 48
CH = VEC * TR * LEV
GROUP = TR * LEV
WCH = NSLAB * 2 * LEV
D = STEPS
EXT = ROWS + 2 * D
PITCH = 80
FIRST = 16
SPAN = 64
WPACK = 896
PART = 640
BLOCK = 88


def place(x, y, z, core):
    return (x * 2 + y % 2) * 16 + (y // 2) * 8 + z * 2 + core


PLACES = [(x, y, z, c) for x in range(4) for y in range(4) for z in range(4) for c in range(2)]


def moved(dx=0, dy=0, dz=0, dc=0):
    return [
        (place(x, y, z, c), place((x + dx) % 4, (y + dy) % 4, (z + dz) % 4, c ^ dc))
        for x, y, z, c in PLACES
    ]


def turned(bits):
    return [(place(x, y, z, c), place(x, y ^ bits, z, c)) for x, y, z, c in PLACES]


def meridian():
    pairs = []
    for b in range(8):
        for a in range(8):
            pairs.append((a * 16 + b, (a + 1) * 16 + b if a < 7 else a * 16 + b + 8))
            pairs.append((a * 16 + b + 8, (a - 1) * 16 + b + 8 if a > 0 else a * 16 + b))
    return pairs


FORWARD = meridian()
BACKWARD = [(t, s) for s, t in FORWARD]
EASTWARD = [(b, (b + 1) % 16) for b in range(16)]
WESTWARD = [(t, s) for s, t in EASTWARD]


def edge_tile(r, m):
    i = r * (CH // 128) + m
    return slice(i // 6 * 8, i // 6 * 8 + 8), slice(WPACK + i % 6 * 128, WPACK + i % 6 * 128 + 128)


def choose(vec_ids, chosen):
    lane = lax.broadcasted_iota(jnp.int32, (1, CH), 1)
    source = lane
    for k in range(VEC):
        inside = (lane >= k * GROUP) & (lane < (k + 1) * GROUP)
        source = jnp.where(inside, lane + (vec_ids[k] - k) * GROUP, source)
    for i in range(CH // 128):
        row = lax.broadcasted_iota(jnp.int32, (128, CH), 0) + i * 128
        chosen[i * 128 : (i + 1) * 128, :] = jnp.where(row == source, 1.0, 0.0).astype(jnp.bfloat16)


def turned_wind(winds, info, r):
    place_in_slab = lax.rem(lax.broadcasted_iota(jnp.int32, (1, WCH), 1), 2 * LEV)
    turn = jnp.where((place_in_slab >= LEV) & (info[0] != 0), -1.0, 1.0)
    return winds[jnp.where(info[0] == 0, r, ROWS - 1 - r)] * turn


def lead_kernel(
    info, vec_ids, pool, winds, edge_next, edge_last, chosen, ends, held_winds, made, sems
):
    fetch = [
        pltpu.make_async_copy(pool.at[:, :16, :], ends.at[0], sems.at[0]),
        pltpu.make_async_copy(pool.at[:, COLS - 16 :, :], ends.at[1], sems.at[1]),
        pltpu.make_async_copy(winds, held_winds, sems.at[2]),
    ]
    for copy in fetch:
        copy.start()
    choose(vec_ids, chosen)
    for copy in fetch:
        copy.wait()
    for i in range(2):
        rows = ends[i].reshape(ROWS * 16, CH)
        picked = jnp.dot(rows, chosen[...], preferred_element_type=jnp.float32)
        made[i] = picked.reshape(ROWS, 16, CH)
    for r in range(4):
        for edge, row in ((edge_last, r), (edge_next, 4 + r)):
            own = jnp.where(info[0] == 0, row, ROWS - 1 - row)
            for m in range(CH // 128):
                lanes = slice(m * 128, (m + 1) * 128)
                where = edge_tile(r, m)
                edge[where[0], where[1]] = jnp.concatenate(
                    [made[0, own, :4, lanes], made[1, own, 12:, lanes]], axis=0
                )
    for r in range(3):
        lanes = slice(r * WCH, (r + 1) * WCH)
        edge_last[:, lanes] = turned_wind(held_winds, info, r)
        edge_next[:, lanes] = turned_wind(held_winds, info, ROWS - 3 + r)


def lead(info, vec_ids, pool, winds):
    vmem = pl.BlockSpec(memory_space=pltpu.VMEM)
    return pl.pallas_call(
        lead_kernel,
        out_shape=[jax.ShapeDtypeStruct((COLS, WPACK + 768), jnp.float32)] * 2,
        in_specs=[pl.BlockSpec(memory_space=pltpu.SMEM)] * 2
        + [pl.BlockSpec(memory_space=pltpu.HBM)] * 2,
        out_specs=[vmem] * 2,
        scratch_shapes=[
            pltpu.VMEM((CH, CH), jnp.bfloat16),
            pltpu.VMEM((2, ROWS, 16, CH), jnp.bfloat16),
            pltpu.VMEM((ROWS, COLS, WCH), jnp.float32),
            pltpu.VMEM((2, ROWS, 16, CH), jnp.float32),
            pltpu.SemaphoreType.DMA((3,)),
        ],
        compiler_params=pltpu.CompilerParams(vmem_limit_bytes=60 << 20),
        cost_estimate=pl.CostEstimate(flops=1 << 30, bytes_accessed=4 << 20, transcendentals=0),
        name="lead",
    )(info, vec_ids, pool, winds)


def pack_kernel(
    info, vec_ids, pool, winds, basis,
    low, high, wind, next_0, next_1, last_0, last_1, basis_main, basis_rest, chosen,
):
    choose(vec_ids, chosen)
    for half in range(2):
        rows = pool[half * 4 : half * 4 + 4].reshape(4 * COLS, CH)
        picked = jnp.dot(rows, chosen[...], preferred_element_type=jnp.float32)
        picked = picked.reshape(4, COLS, CH)

        @pl.when(info[0] == 0)
        def _():
            (low, high)[half][...] = picked

        @pl.when(info[0] != 0)
        def _():
            for r in range(4):
                (high, low)[half][3 - r] = picked[r]

    for rows, bulk_0, bulk_1 in ((high, next_0, next_1), (low, last_0, last_1)):
        for r in range(4):
            bulk_0[r] = rows[r, 4 : COLS - 4, :PART]
            bulk_1[r] = rows[r, 4 : COLS - 4, PART:]
    for r in range(ROWS):
        wind[r] = turned_wind(winds, info, r)
    flat = basis[...].reshape(ROWS * COLS, CH)
    for a in range(8):
        basis_main[:, a * 128 : (a + 1) * 128] = flat[:, a * 144 : a * 144 + 128]
        basis_rest[:, a * 16 : (a + 1) * 16] = flat[:, a * 144 + 128 : (a + 1) * 144]


def pack(info, vec_ids, pool, winds, basis):
    shapes = [(4, COLS, CH)] * 2 + [(ROWS, COLS, WCH)]
    shapes += [(4, COLS - 8, PART), (4, COLS - 8, CH - PART)] * 2
    outs = [jax.ShapeDtypeStruct(s, jnp.float32) for s in shapes]
    outs += [jax.ShapeDtypeStruct((ROWS * COLS, n), jnp.bfloat16) for n in (1024, 128)]
    vmem = pl.BlockSpec(memory_space=pltpu.VMEM)
    return pl.pallas_call(
        pack_kernel,
        out_shape=outs,
        in_specs=[pl.BlockSpec(memory_space=pltpu.SMEM)] * 2 + [vmem] * 3,
        out_specs=[vmem] * 9,
        scratch_shapes=[pltpu.VMEM((CH, CH), jnp.bfloat16)],
        compiler_params=pltpu.CompilerParams(vmem_limit_bytes=24 << 20),
        cost_estimate=pl.CostEstimate(flops=1 << 30, bytes_accessed=4 << 20, transcendentals=0),
        name="pack",
    )(info, vec_ids, pool, winds, basis)


SIDE = EXT - 2


def edges_kernel(before, after, low, high, wind, *rest):
    to_east, to_west = rest[4:6]
    for first, near, target in ((COLS - 4, 4, to_east), (0, 0, to_west)):
        columns = slice(first, first + 4)
        for r in range(3):
            for m in range(CH // 128):
                lanes = slice(m * 128, (m + 1) * 128)
                where = edge_tile(r + 1, m)
                target[r, :, lanes] = before[where[0], where[1]][near : near + 4]
                where = edge_tile(r, m)
                target[11 + r, :, lanes] = after[where[0], where[1]][near : near + 4]
        for r in range(4):
            target[3 + r] = low[r, columns, :]
            target[7 + r] = high[r, columns, :]
        for r in range(SIDE):
            if r < 3:
                line = before[columns, r * WCH : (r + 1) * WCH]
            elif r < 11:
                line = wind[r - 3, columns, :]
            else:
                line = after[columns, (r - 11) * WCH : (r - 10) * WCH]
            target[SIDE + r // 4, :, r % 4 * WCH : (r % 4 + 1) * WCH] = line


def edges(arrays, bulk):
    vmem = pl.BlockSpec(memory_space=pltpu.VMEM)
    anywhere = pl.BlockSpec(memory_space=pl.ANY)
    shapes = [jax.ShapeDtypeStruct((SIDE + 4, 4, CH), jnp.float32)] * 2
    return pl.pallas_call(
        edges_kernel,
        out_shape=shapes + [jax.ShapeDtypeStruct(b.shape, b.dtype) for b in bulk],
        in_specs=[vmem] * 5 + [anywhere] * 4,
        out_specs=[vmem] * 2 + [anywhere] * 4,
        input_output_aliases={5 + i: 2 + i for i in range(4)},
        compiler_params=pltpu.CompilerParams(vmem_limit_bytes=16 << 20),
        cost_estimate=pl.CostEstimate(flops=1 << 20, bytes_accessed=4 << 20, transcendentals=0),
        name="edges",
    )(*arrays, *bulk)


def frame_kernel(info, before, after, wind, west, east, wind_ext):
    turn_west, turn_east = info[5], info[6]
    for r in range(3):
        lanes = slice(r * WCH, (r + 1) * WCH)
        wind_ext[r, 8 : 8 + COLS] = before[:, lanes]
        wind_ext[11 + r, 8 : 8 + COLS] = after[:, lanes]
    for r in range(ROWS):
        wind_ext[3 + r, 8 : 8 + COLS] = wind[r]
    lane = lax.rem(lax.broadcasted_iota(jnp.int32, (1, WCH), 1), 2 * LEV)
    for turn, payload, first in ((turn_west, west, 4), (turn_east, east, 8 + COLS)):
        sign = jnp.where((lane >= LEV) & (turn != 0), -1.0, 1.0)
        for r in range(SIDE):
            line = payload[SIDE + r // 4, :, r % 4 * WCH : (r % 4 + 1) * WCH] * sign
            wind_ext[jnp.where(turn == 0, r, SIDE - 1 - r), first : first + 4] = line


def frame_winds(info, *arrays):
    vmem = pl.BlockSpec(memory_space=pltpu.VMEM)
    return pl.pallas_call(
        frame_kernel,
        out_shape=jax.ShapeDtypeStruct((SIDE, SPAN, WCH), jnp.float32),
        in_specs=[pl.BlockSpec(memory_space=pltpu.SMEM)] + [vmem] * 5,
        out_specs=vmem,
        compiler_params=pltpu.CompilerParams(vmem_limit_bytes=16 << 20),
        cost_estimate=pl.CostEstimate(flops=16 << 30, bytes_accessed=4 << 20, transcendentals=0),
        name="frame",
    )(info, *arrays)


def window_kernel(
    part, info, wind_ids, cosine,
    before_edge, low, high, after_edge, west, east, wind_ext,
    levels, mix, basis_main, basis_rest, before_0, after_0,
    *others,
):
    before_1, after_1, earlier = others[:3] if part else (None, None, None)
    out, mine, theirs, state_a, state_b, spread, weighted, gram, rest = others[3 * part :]
    flip, mx, my, mz, mc, turn_west, turn_east = (info[i] for i in range(7))
    lanes = slice(part * 512, part * 512 + PART)
    skip = part * 64

    for r in range(4):
        state_a[4 + r, FIRST : FIRST + COLS] = low[r, :, lanes]
        state_a[8 + r, FIRST : FIRST + COLS] = high[r, :, lanes]
        for row, edge, bulk_0, bulk_1 in (
            (r, before_edge, before_0, before_1),
            (12 + r, after_edge, after_0, after_1),
        ):
            middle = slice(FIRST + 4, FIRST + COLS - 4)
            if part:
                state_a[row, middle, :128] = bulk_0[r, :, 512:]
                state_a[row, middle, 128:] = bulk_1[r]
            else:
                state_a[row, middle] = bulk_0[r]
            for m in range(PART // 128):
                tile = slice(m * 128, (m + 1) * 128)
                where = edge_tile(r, m + part * 4)
                ends = edge[where[0], where[1]]
                state_a[row, FIRST : FIRST + 4, tile] = ends[:4]
                state_a[row, FIRST + COLS - 4 : FIRST + COLS, tile] = ends[4:]
    for r in range(SIDE):
        from_west = jnp.where(turn_west == 0, r, SIDE - 1 - r)
        from_east = jnp.where(turn_east == 0, r, SIDE - 1 - r)
        state_a[1 + r, FIRST - 4 : FIRST] = west[from_west, :, lanes]
        state_a[1 + r, FIRST + COLS : FIRST + COLS + 4] = east[from_east, :, lanes]

    level = lax.broadcasted_iota(jnp.int32, (2 * LEV, PART), 0)
    level = jnp.where(level >= LEV, level - LEV, level)
    repeat = jnp.where(level == levels[:, lanes], 1.0, 0.0).astype(jnp.bfloat16)
    flat = wind_ext[...].reshape(SIDE * SPAN, WCH)
    for i in range(2 * NSLAB):
        value = flat[:, i * LEV : (i + 1) * LEV]
        coarse = value.astype(jnp.bfloat16)
        fine = (value - coarse.astype(jnp.float32)).astype(jnp.bfloat16)
        both = jnp.concatenate([coarse, fine], axis=1)
        spread[i] = jnp.dot(both, repeat, preferred_element_type=jnp.float32).reshape(
            SIDE, SPAN, PART
        )

    up, down = mix[0:1, lanes], mix[1:2, lanes]

    def updated(source, slab, r, c):
        now = source[r, pl.ds(c, 8), :]
        after = source[r + 1, pl.ds(c, 8), :]
        before = source[r - 1, pl.ds(c, 8), :]
        east_side = source[r, pl.ds(c + 1, 8), :]
        west_side = source[r, pl.ds(c - 1, 8), :]
        u = spread[2 * slab, r - 1, pl.ds(c - FIRST + 8, 8), :]
        v = spread[2 * slab + 1, r - 1, pl.ds(c - FIRST + 8, 8), :]
        gain_east = jnp.maximum(u, 0.0) + DIFFUSE
        gain_after = jnp.maximum(v, 0.0) + DIFFUSE
        change = gain_east * (east_side - now) + (gain_east - u) * (west_side - now)
        change += gain_after * (after - now) + (gain_after - v) * (before - now)
        above, below = pltpu.roll(now, PART - 1, 1), pltpu.roll(now, 1, 1)
        change += up * (above - now) - down * (now - below)
        return now + change

    buffers = (state_a, state_b)
    for step in range(STEPS - 1):
        source, target = buffers[step % 2], buffers[(step + 1) % 2]
        slab = wind_ids[step]

        def body(r, carry):
            for c in range(FIRST - 8, FIRST - 8 + SPAN, 8):
                target[r, c : c + 8, :] = updated(source, slab, r, c)
            return carry

        lax.fori_loop(1 + step, EXT - 1 - step, body, 0)

    source = buffers[(STEPS - 1) % 2]
    slab = wind_ids[STEPS - 1]
    own_lanes = lax.broadcasted_iota(jnp.int32, (16, 128), 1) >= skip

    def last(r, carry):
        own = jnp.where(flip == 0, r - D, ROWS - 1 - (r - D))
        share = cosine[own]
        for c in range(0, COLS, 16):
            first = updated(source, slab, r, FIRST + c)
            second = updated(source, slab, r, FIRST + c + 8)
            both = jnp.concatenate([first, second], axis=0)
            if part:
                there = slice(c, c + 16)
                out[own, there, :512] = earlier[own, there, :512]
                out[own, there, 512:640] = jnp.where(
                    own_lanes, both[:, :128], earlier[own, there, 512:]
                )
                out[own, there, 640:] = both[:, 128:]
            else:
                out[own, c : c + 16, :] = both
            weighted[own, c : c + 16, :] = (both * share).astype(jnp.bfloat16)
        return carry

    lax.fori_loop(D, D + ROWS, last, 0)

    flat_weighted = weighted[...].reshape(ROWS * COLS, PART)
    across = (((0,), (0,)), ((), ()))
    for i in range(PART // 128):
        gram[i * 128 : (i + 1) * 128, :] = lax.dot_general(
            flat_weighted[:, i * 128 : (i + 1) * 128],
            basis_main[...],
            across,
            preferred_element_type=jnp.float32,
        )
    tail = lax.dot_general(
        basis_rest[...], flat_weighted, across, preferred_element_type=jnp.float32
    )
    for g in range(8):
        rest[g, :, :LEV] = tail[:, skip + g * LEV : skip + (g + 1) * LEV]

    def place_blocks(i, carry):
        rz, rx, ry = i // 8, (i // 2) % 4, i % 2
        z, x = (mz + rz) % 4, (mx + rx) % 4
        outer, inner = (rx, rz) if part else (rz, rx)
        at = outer * 8 + inner * 2 + ry
        a = x * 2 + (my ^ ry)
        for dc, target in ((0, mine), (1, theirs)):
            g = z * 2 + (mc ^ dc)
            target[at, :LEV] = gram[
                pl.ds(pl.multiple_of(skip + g * LEV, 8), LEV),
                pl.ds(pl.multiple_of(a * 128, 128), 128),
            ]
            target[at, LEV:] = rest[g, pl.ds(pl.multiple_of(a * 16, 16), 16), :]
        return carry

    lax.fori_loop(0, 32, place_blocks, 0, unroll=4)


def window(part, scalars, arrays):
    blocks = jax.ShapeDtypeStruct((32, BLOCK, 128), jnp.float32)
    vmem = pl.BlockSpec(memory_space=pltpu.VMEM)
    return pl.pallas_call(
        functools.partial(window_kernel, part),
        out_shape=[
            jax.ShapeDtypeStruct((ROWS, COLS, CH if part else PART), jnp.float32),
            blocks,
            blocks,
        ],
        in_specs=[pl.BlockSpec(memory_space=pltpu.SMEM)] * len(scalars) + [vmem] * len(arrays),
        out_specs=[vmem] * 3,
        scratch_shapes=[
            pltpu.VMEM((EXT, PITCH, PART), jnp.float32),
            pltpu.VMEM((EXT, PITCH, PART), jnp.float32),
            pltpu.VMEM((2 * NSLAB, SIDE, SPAN, PART), jnp.float32),
            pltpu.VMEM((ROWS, COLS, PART), jnp.bfloat16),
            pltpu.VMEM((PART, 1024), jnp.float32),
            pltpu.VMEM((8, 128, 128), jnp.float32),
        ],
        compiler_params=pltpu.CompilerParams(vmem_limit_bytes=40 << 20),
        cost_estimate=pl.CostEstimate(flops=8 << 30, bytes_accessed=16 << 20, transcendentals=0),
        name=f"window_{part}",
    )(*scalars, *arrays)


def line_sum(parts, **axis):
    (name,) = axis
    sent = [lax.ppermute(parts[k], ALL, moved(**{name: k})) for k in (1, 2, 3)]
    return (parts[0] + sent[0]) + (sent[1] + sent[2])


def shards(pool, vec_ids, winds, wind_ids, mixing, basis):
    lat_index = lax.axis_index("lat").astype(jnp.int32)
    lon_index = lax.axis_index("lon").astype(jnp.int32)
    flip = lon_index // 8
    info = jnp.stack(
        [
            flip,
            lat_index // 2,
            lat_index % 2,
            (lon_index // 2) % 4,
            lon_index % 2,
            (lon_index % 8 == 0).astype(jnp.int32),
            (lon_index % 8 == 7).astype(jnp.int32),
        ]
    )
    edge_next, edge_last = lead(info, vec_ids, pool, winds)
    before_edge = lax.ppermute(edge_next, ALL, FORWARD)
    after_edge = lax.ppermute(edge_last, ALL, BACKWARD)
    low, high, wind, next_0, next_1, last_0, last_1, basis_main, basis_rest = pack(
        info, vec_ids, pool, winds, basis
    )
    to_east, to_west, *bulk = edges(
        (before_edge, after_edge, low, high, wind), (next_0, last_0, next_1, last_1)
    )
    west = lax.ppermute(to_east, "lon", EASTWARD)
    east = lax.ppermute(to_west, "lon", WESTWARD)
    before_0, after_0 = lax.ppermute(bulk[0], ALL, FORWARD), lax.ppermute(bulk[1], ALL, BACKWARD)
    before_1, after_1 = lax.ppermute(bulk[2], ALL, FORWARD), lax.ppermute(bulk[3], ALL, BACKWARD)
    wind_ext = frame_winds(info, before_edge, after_edge, wind, west, east)

    level_mix = jnp.concatenate(
        [mixing.reshape(TR, LEV - 1), jnp.zeros((TR, 1), mixing.dtype)], axis=1
    )
    upper = jnp.tile(level_mix.reshape(GROUP), VEC)
    mix = jnp.stack([upper, jnp.roll(upper, 1)])
    rows = (jnp.arange(ROWS, dtype=jnp.int32) + lat_index * ROWS).astype(jnp.float32)
    cosine = jnp.cos((rows + 0.5) * (math.pi / (ROWS * 8)) - math.pi / 2)
    levels = jnp.asarray(np.arange(CH, dtype=np.int32)[None] % LEV)
    scalars = (info, wind_ids, cosine)
    arrays = (
        before_edge, low, high, after_edge, west, east, wind_ext,
        levels, mix, basis_main, basis_rest, before_0, after_0,
    )
    half, mine, theirs = window(0, scalars, arrays)
    first = mine + lax.ppermute(theirs, ALL, moved(dc=1))
    sensitivity, mine, theirs = window(1, scalars, (*arrays, before_1, after_1, half))
    second = mine + lax.ppermute(theirs, ALL, moved(dc=1))

    first = line_sum(first.reshape(4, 8, BLOCK, 128), dz=1)
    second = line_sum(second.reshape(4, 8, BLOCK, 128), dx=1)
    first = line_sum(first.reshape(4, 2, BLOCK, 128), dx=1)
    second = line_sum(second.reshape(4, 2, BLOCK, 128), dz=1)
    near = jnp.where(flip == 0, first, second)
    far = jnp.where(flip == 0, second, first)
    block = near[0] + lax.ppermute(near[1], ALL, turned(1))
    block += lax.ppermute(far[0], ALL, turned(2)) + lax.ppermute(far[1], ALL, turned(3))
    ritz = jnp.concatenate([block[:LEV].T, block[LEV:, :LEV]], axis=0)
    return sensitivity, ritz * (1.0 / math.sqrt(ROWS * COLS * 128))


def solution(mesh):
    in_specs = (P("lat", "lon", None), P(), P("lat", "lon", None), P(), P(), P("lat", "lon", None))
    out_specs = (P("lat", "lon", None), P("lat", "lon"))
    return jax.shard_map(shards, mesh=mesh, in_specs=in_specs, out_specs=out_specs, check_vma=False)
```

```python
import functools
import functools
import math

import jax
import jax.numpy as jnp
import numpy as np
from jax import lax
from jax.experimental import pallas as pl
from jax.experimental.pallas import tpu as pltpu
from jax.sharding import PartitionSpec as P

LEV = 72
TR = 2
VEC = 8
POOL = 8
NSLAB = 2
STEPS = 4
DIFFUSE = 0.075
ALL = ("lat", "lon")

ROWS = 8
COLS = 48
CH = VEC * TR * LEV
GROUP = TR * LEV
WCH = NSLAB * 2 * LEV
D = STEPS
EXT = ROWS + 2 * D
PITCH = 80
FIRST = 16
SPAN = 64
WPACK = 896
PART = 640
BLOCK = 88


def place(x, y, z, core):
    return (x * 2 + y % 2) * 16 + (y // 2) * 8 + z * 2 + core


PLACES = [(x, y, z, c) for x in range(4) for y in range(4) for z in range(4) for c in range(2)]


def moved(dx=0, dy=0, dz=0, dc=0):
    return [
        (place(x, y, z, c), place((x + dx) % 4, (y + dy) % 4, (z + dz) % 4, c ^ dc))
        for x, y, z, c in PLACES
    ]


def turned(bits):
    return [(place(x, y, z, c), place(x, y ^ bits, z, c)) for x, y, z, c in PLACES]


def meridian():
    pairs = []
    for b in range(8):
        for a in range(8):
            pairs.append((a * 16 + b, (a + 1) * 16 + b if a < 7 else a * 16 + b + 8))
            pairs.append((a * 16 + b + 8, (a - 1) * 16 + b + 8 if a > 0 else a * 16 + b))
    return pairs


FORWARD = meridian()
BACKWARD = [(t, s) for s, t in FORWARD]
EASTWARD = [(b, (b + 1) % 16) for b in range(16)]
WESTWARD = [(t, s) for s, t in EASTWARD]


def edge_tile(r, m):
    i = r * (CH // 128) + m
    return slice(i // 6 * 8, i // 6 * 8 + 8), slice(WPACK + i % 6 * 128, WPACK + i % 6 * 128 + 128)


def choose(vec_ids, chosen):
    lane = lax.broadcasted_iota(jnp.int32, (1, CH), 1)
    source = lane
    for k in range(VEC):
        inside = (lane >= k * GROUP) & (lane < (k + 1) * GROUP)
        source = jnp.where(inside, lane + (vec_ids[k] - k) * GROUP, source)
    for i in range(CH // 128):
        row = lax.broadcasted_iota(jnp.int32, (128, CH), 0) + i * 128
        chosen[i * 128 : (i + 1) * 128, :] = jnp.where(row == source, 1.0, 0.0).astype(jnp.bfloat16)


def turned_wind(winds, info, r):
    place_in_slab = lax.rem(lax.broadcasted_iota(jnp.int32, (1, WCH), 1), 2 * LEV)
    turn = jnp.where((place_in_slab >= LEV) & (info[0] != 0), -1.0, 1.0)
    return winds[jnp.where(info[0] == 0, r, ROWS - 1 - r)] * turn


def lead_kernel(
    info, vec_ids, pool, winds, edge_next, edge_last, chosen, ends, held_winds, made, sems
):
    fetch = [
        pltpu.make_async_copy(pool.at[:, :16, :], ends.at[0], sems.at[0]),
        pltpu.make_async_copy(pool.at[:, COLS - 16 :, :], ends.at[1], sems.at[1]),
        pltpu.make_async_copy(winds, held_winds, sems.at[2]),
    ]
    for copy in fetch:
        copy.start()
    choose(vec_ids, chosen)
    for copy in fetch:
        copy.wait()
    for i in range(2):
        rows = ends[i].reshape(ROWS * 16, CH)
        picked = jnp.dot(rows, chosen[...], preferred_element_type=jnp.float32)
        made[i] = picked.reshape(ROWS, 16, CH)
    for r in range(4):
        for edge, row in ((edge_last, r), (edge_next, 4 + r)):
            own = jnp.where(info[0] == 0, row, ROWS - 1 - row)
            for m in range(CH // 128):
                lanes = slice(m * 128, (m + 1) * 128)
                where = edge_tile(r, m)
                edge[where[0], where[1]] = jnp.concatenate(
                    [made[0, own, :4, lanes], made[1, own, 12:, lanes]], axis=0
                )
    for r in range(3):
        lanes = slice(r * WCH, (r + 1) * WCH)
        edge_last[:, lanes] = turned_wind(held_winds, info, r)
        edge_next[:, lanes] = turned_wind(held_winds, info, ROWS - 3 + r)


def lead(info, vec_ids, pool, winds):
    vmem = pl.BlockSpec(memory_space=pltpu.VMEM)
    return pl.pallas_call(
        lead_kernel,
        out_shape=[jax.ShapeDtypeStruct((COLS, WPACK + 768), jnp.float32)] * 2,
        in_specs=[pl.BlockSpec(memory_space=pltpu.SMEM)] * 2
        + [pl.BlockSpec(memory_space=pltpu.HBM)] * 2,
        out_specs=[vmem] * 2,
        scratch_shapes=[
            pltpu.VMEM((CH, CH), jnp.bfloat16),
            pltpu.VMEM((2, ROWS, 16, CH), jnp.bfloat16),
            pltpu.VMEM((ROWS, COLS, WCH), jnp.float32),
            pltpu.VMEM((2, ROWS, 16, CH), jnp.float32),
            pltpu.SemaphoreType.DMA((3,)),
        ],
        compiler_params=pltpu.CompilerParams(vmem_limit_bytes=60 << 20),
        cost_estimate=pl.CostEstimate(flops=1 << 30, bytes_accessed=4 << 20, transcendentals=0),
        name="lead",
    )(info, vec_ids, pool, winds)


def pack_kernel(
    info, vec_ids, pool, winds, basis,
    low, high, wind, next_0, next_1, last_0, last_1, basis_main, basis_rest, chosen,
):
    choose(vec_ids, chosen)
    for half in range(2):
        rows = pool[half * 4 : half * 4 + 4].reshape(4 * COLS, CH)
        picked = jnp.dot(rows, chosen[...], preferred_element_type=jnp.float32)
        picked = picked.reshape(4, COLS, CH)

        @pl.when(info[0] == 0)
        def _():
            (low, high)[half][...] = picked

        @pl.when(info[0] != 0)
        def _():
            for r in range(4):
                (high, low)[half][3 - r] = picked[r]

    for rows, bulk_0, bulk_1 in ((high, next_0, next_1), (low, last_0, last_1)):
        for r in range(4):
            bulk_0[r] = rows[r, 4 : COLS - 4, :PART]
            bulk_1[r] = rows[r, 4 : COLS - 4, PART:]
    for r in range(ROWS):
        wind[r] = turned_wind(winds, info, r)
    flat = basis[...].reshape(ROWS * COLS, CH)
    for a in range(8):
        basis_main[:, a * 128 : (a + 1) * 128] = flat[:, a * 144 : a * 144 + 128]
        basis_rest[:, a * 16 : (a + 1) * 16] = flat[:, a * 144 + 128 : (a + 1) * 144]


def pack(info, vec_ids, pool, winds, basis):
    shapes = [(4, COLS, CH)] * 2 + [(ROWS, COLS, WCH)]
    shapes += [(4, COLS - 8, PART), (4, COLS - 8, CH - PART)] * 2
    outs = [jax.ShapeDtypeStruct(s, jnp.float32) for s in shapes]
    outs += [jax.ShapeDtypeStruct((ROWS * COLS, n), jnp.bfloat16) for n in (1024, 128)]
    vmem = pl.BlockSpec(memory_space=pltpu.VMEM)
    return pl.pallas_call(
        pack_kernel,
        out_shape=outs,
        in_specs=[pl.BlockSpec(memory_space=pltpu.SMEM)] * 2 + [vmem] * 3,
        out_specs=[vmem] * 9,
        scratch_shapes=[pltpu.VMEM((CH, CH), jnp.bfloat16)],
        compiler_params=pltpu.CompilerParams(vmem_limit_bytes=24 << 20),
        cost_estimate=pl.CostEstimate(flops=1 << 30, bytes_accessed=4 << 20, transcendentals=0),
        name="pack",
    )(info, vec_ids, pool, winds, basis)


SIDE = EXT - 2


def edges_kernel(before, after, low, high, wind, *rest):
    to_east, to_west = rest[4:6]
    for first, near, target in ((COLS - 4, 4, to_east), (0, 0, to_west)):
        columns = slice(first, first + 4)
        for r in range(3):
            for m in range(CH // 128):
                lanes = slice(m * 128, (m + 1) * 128)
                where = edge_tile(r + 1, m)
                target[r, :, lanes] = before[where[0], where[1]][near : near + 4]
                where = edge_tile(r, m)
                target[11 + r, :, lanes] = after[where[0], where[1]][near : near + 4]
        for r in range(4):
            target[3 + r] = low[r, columns, :]
            target[7 + r] = high[r, columns, :]
        for r in range(SIDE):
            if r < 3:
                line = before[columns, r * WCH : (r + 1) * WCH]
            elif r < 11:
                line = wind[r - 3, columns, :]
            else:
                line = after[columns, (r - 11) * WCH : (r - 10) * WCH]
            target[SIDE + r // 4, :, r % 4 * WCH : (r % 4 + 1) * WCH] = line


def edges(arrays, bulk):
    vmem = pl.BlockSpec(memory_space=pltpu.VMEM)
    anywhere = pl.BlockSpec(memory_space=pl.ANY)
    shapes = [jax.ShapeDtypeStruct((SIDE + 4, 4, CH), jnp.float32)] * 2
    return pl.pallas_call(
        edges_kernel,
        out_shape=shapes + [jax.ShapeDtypeStruct(b.shape, b.dtype) for b in bulk],
        in_specs=[vmem] * 5 + [anywhere] * 4,
        out_specs=[vmem] * 2 + [anywhere] * 4,
        input_output_aliases={5 + i: 2 + i for i in range(4)},
        compiler_params=pltpu.CompilerParams(vmem_limit_bytes=16 << 20),
        cost_estimate=pl.CostEstimate(flops=1 << 20, bytes_accessed=4 << 20, transcendentals=0),
        name="edges",
    )(*arrays, *bulk)


def repeat_winds(wind_ext, levels, lanes, spread):
    level = lax.broadcasted_iota(jnp.int32, (2 * LEV, PART), 0)
    level = jnp.where(level >= LEV, level - LEV, level)
    repeat = jnp.where(level == levels[:, lanes], 1.0, 0.0).astype(jnp.bfloat16)
    flat = wind_ext[...].reshape(SIDE * SPAN, WCH)
    for i in range(2 * NSLAB):
        value = flat[:, i * LEV : (i + 1) * LEV]
        coarse = value.astype(jnp.bfloat16)
        fine = (value - coarse.astype(jnp.float32)).astype(jnp.bfloat16)
        both = jnp.concatenate([coarse, fine], axis=1)
        spread[i] = jnp.dot(both, repeat, preferred_element_type=jnp.float32).reshape(
            SIDE, SPAN, PART
        )


def frame_kernel(info, before, after, wind, west, east, levels, wind_ext, spread):
    turn_west, turn_east = info[5], info[6]
    for r in range(3):
        lanes = slice(r * WCH, (r + 1) * WCH)
        wind_ext[r, 8 : 8 + COLS] = before[:, lanes]
        wind_ext[11 + r, 8 : 8 + COLS] = after[:, lanes]
    for r in range(ROWS):
        wind_ext[3 + r, 8 : 8 + COLS] = wind[r]
    lane = lax.rem(lax.broadcasted_iota(jnp.int32, (1, WCH), 1), 2 * LEV)
    for turn, payload, first in ((turn_west, west, 4), (turn_east, east, 8 + COLS)):
        sign = jnp.where((lane >= LEV) & (turn != 0), -1.0, 1.0)
        for r in range(SIDE):
            line = payload[SIDE + r // 4, :, r % 4 * WCH : (r % 4 + 1) * WCH] * sign
            wind_ext[jnp.where(turn == 0, r, SIDE - 1 - r), first : first + 4] = line
    repeat_winds(wind_ext, levels, slice(512, 512 + PART), spread)


def frame_winds(info, *arrays):
    vmem = pl.BlockSpec(memory_space=pltpu.VMEM)
    return pl.pallas_call(
        frame_kernel,
        out_shape=[
            jax.ShapeDtypeStruct((SIDE, SPAN, WCH), jnp.float32),
            jax.ShapeDtypeStruct((2 * NSLAB, SIDE, SPAN, PART), jnp.float32),
        ],
        in_specs=[pl.BlockSpec(memory_space=pltpu.SMEM)] + [vmem] * 6,
        out_specs=[vmem] * 2,
        compiler_params=pltpu.CompilerParams(vmem_limit_bytes=24 << 20),
        cost_estimate=pl.CostEstimate(flops=16 << 30, bytes_accessed=4 << 20, transcendentals=0),
        name="frame",
    )(info, *arrays)


def window_kernel(
    part, info, wind_ids, cosine,
    before_edge, low, high, after_edge, west, east, wind_ext,
    levels, mix, basis_main, basis_rest, before_0, after_0,
    *others,
):
    before_1, after_1, earlier = others[:3] if part else (None, None, None)
    out, mine, theirs, state_a, state_b, weighted, gram, rest, *spread = others[3 * part :]
    spread = spread[0] if spread else None
    flip, mx, my, mz, mc, turn_west, turn_east = (info[i] for i in range(7))
    lanes = slice(part * 512, part * 512 + PART)
    skip = part * 64

    for r in range(4):
        state_a[4 + r, FIRST : FIRST + COLS] = low[r, :, lanes]
        state_a[8 + r, FIRST : FIRST + COLS] = high[r, :, lanes]
        for row, edge, bulk_0, bulk_1 in (
            (r, before_edge, before_0, before_1),
            (12 + r, after_edge, after_0, after_1),
        ):
            middle = slice(FIRST + 4, FIRST + COLS - 4)
            if part:
                state_a[row, middle, :128] = bulk_0[r, :, 512:]
                state_a[row, middle, 128:] = bulk_1[r]
            else:
                state_a[row, middle] = bulk_0[r]
            for m in range(PART // 128):
                tile = slice(m * 128, (m + 1) * 128)
                where = edge_tile(r, m + part * 4)
                ends = edge[where[0], where[1]]
                state_a[row, FIRST : FIRST + 4, tile] = ends[:4]
                state_a[row, FIRST + COLS - 4 : FIRST + COLS, tile] = ends[4:]
    for r in range(SIDE):
        from_west = jnp.where(turn_west == 0, r, SIDE - 1 - r)
        from_east = jnp.where(turn_east == 0, r, SIDE - 1 - r)
        state_a[1 + r, FIRST - 4 : FIRST] = west[from_west, :, lanes]
        state_a[1 + r, FIRST + COLS : FIRST + COLS + 4] = east[from_east, :, lanes]

    if part:
        spread = wind_ext
    else:
        repeat_winds(wind_ext, levels, lanes, spread)

    up, down = mix[0:1, lanes], mix[1:2, lanes]

    def updated(source, slab, r, c):
        now = source[r, pl.ds(c, 8), :]
        after = source[r + 1, pl.ds(c, 8), :]
        before = source[r - 1, pl.ds(c, 8), :]
        east_side = source[r, pl.ds(c + 1, 8), :]
        west_side = source[r, pl.ds(c - 1, 8), :]
        u = spread[2 * slab, r - 1, pl.ds(c - FIRST + 8, 8), :]
        v = spread[2 * slab + 1, r - 1, pl.ds(c - FIRST + 8, 8), :]
        gain_east = jnp.maximum(u, 0.0) + DIFFUSE
        gain_after = jnp.maximum(v, 0.0) + DIFFUSE
        change = gain_east * (east_side - now) + (gain_east - u) * (west_side - now)
        change += gain_after * (after - now) + (gain_after - v) * (before - now)
        above, below = pltpu.roll(now, PART - 1, 1), pltpu.roll(now, 1, 1)
        change += up * (above - now) - down * (now - below)
        return now + change

    buffers = (state_a, state_b)
    for step in range(STEPS - 1):
        source, target = buffers[step % 2], buffers[(step + 1) % 2]
        slab = wind_ids[step]

        def body(r, carry):
            for c in range(FIRST - 8, FIRST - 8 + SPAN, 8):
                target[r, c : c + 8, :] = updated(source, slab, r, c)
            return carry

        lax.fori_loop(1 + step, EXT - 1 - step, body, 0)

    source = buffers[(STEPS - 1) % 2]
    slab = wind_ids[STEPS - 1]
    own_lanes = lax.broadcasted_iota(jnp.int32, (16, 128), 1) >= skip

    def last(r, carry):
        own = jnp.where(flip == 0, r - D, ROWS - 1 - (r - D))
        share = cosine[own]
        for c in range(0, COLS, 16):
            first = updated(source, slab, r, FIRST + c)
            second = updated(source, slab, r, FIRST + c + 8)
            both = jnp.concatenate([first, second], axis=0)
            if part:
                there = slice(c, c + 16)
                out[own, there, :512] = earlier[own, there, :512]
                out[own, there, 512:640] = jnp.where(
                    own_lanes, both[:, :128], earlier[own, there, 512:]
                )
                out[own, there, 640:] = both[:, 128:]
            else:
                out[own, c : c + 16, :] = both
            weighted[own, c : c + 16, :] = (both * share).astype(jnp.bfloat16)
        return carry

    lax.fori_loop(D, D + ROWS, last, 0)

    flat_weighted = weighted[...].reshape(ROWS * COLS, PART)
    across = (((0,), (0,)), ((), ()))
    for i in range(PART // 128):
        gram[i * 128 : (i + 1) * 128, :] = lax.dot_general(
            flat_weighted[:, i * 128 : (i + 1) * 128],
            basis_main[...],
            across,
            preferred_element_type=jnp.float32,
        )
    tail = lax.dot_general(
        basis_rest[...], flat_weighted, across, preferred_element_type=jnp.float32
    )
    for g in range(8):
        rest[g, :, :LEV] = tail[:, skip + g * LEV : skip + (g + 1) * LEV]

    def place_blocks(i, carry):
        rz, rx, ry = i // 8, (i // 2) % 4, i % 2
        z, x = (mz + rz) % 4, (mx + rx) % 4
        outer, inner = (rx, rz) if part else (rz, rx)
        at = outer * 8 + inner * 2 + ry
        a = x * 2 + (my ^ ry)
        for dc, target in ((0, mine), (1, theirs)):
            g = z * 2 + (mc ^ dc)
            target[at, :LEV] = gram[
                pl.ds(pl.multiple_of(skip + g * LEV, 8), LEV),
                pl.ds(pl.multiple_of(a * 128, 128), 128),
            ]
            target[at, LEV:] = rest[g, pl.ds(pl.multiple_of(a * 16, 16), 16), :]
        return carry

    lax.fori_loop(0, 32, place_blocks, 0, unroll=8)


def window(part, scalars, arrays):
    blocks = jax.ShapeDtypeStruct((32, BLOCK, 128), jnp.float32)
    vmem = pl.BlockSpec(memory_space=pltpu.VMEM)
    return pl.pallas_call(
        functools.partial(window_kernel, part),
        out_shape=[
            jax.ShapeDtypeStruct((ROWS, COLS, CH if part else PART), jnp.float32),
            blocks,
            blocks,
        ],
        in_specs=[pl.BlockSpec(memory_space=pltpu.SMEM)] * len(scalars) + [vmem] * len(arrays),
        out_specs=[vmem] * 3,
        scratch_shapes=[
            pltpu.VMEM((EXT, PITCH, PART), jnp.float32),
            pltpu.VMEM((EXT, PITCH, PART), jnp.float32),
            pltpu.VMEM((ROWS, COLS, PART), jnp.bfloat16),
            pltpu.VMEM((PART, 1024), jnp.float32),
            pltpu.VMEM((8, 128, 128), jnp.float32),
        ]
        + [pltpu.VMEM((2 * NSLAB, SIDE, SPAN, PART), jnp.float32)] * (1 - part),
        compiler_params=pltpu.CompilerParams(vmem_limit_bytes=(24 if part else 32) << 20),
        cost_estimate=pl.CostEstimate(flops=8 << 30, bytes_accessed=16 << 20, transcendentals=0),
        name=f"window_{part}",
    )(*scalars, *arrays)


def line_sum(parts, **axis):
    (name,) = axis
    sent = [lax.ppermute(parts[k], ALL, moved(**{name: k})) for k in (1, 2, 3)]
    return (parts[0] + sent[0]) + (sent[1] + sent[2])


def shards(pool, vec_ids, winds, wind_ids, mixing, basis):
    lat_index = lax.axis_index("lat").astype(jnp.int32)
    lon_index = lax.axis_index("lon").astype(jnp.int32)
    flip = lon_index // 8
    info = jnp.stack(
        [
            flip,
            lat_index // 2,
            lat_index % 2,
            (lon_index // 2) % 4,
            lon_index % 2,
            (lon_index % 8 == 0).astype(jnp.int32),
            (lon_index % 8 == 7).astype(jnp.int32),
        ]
    )
    edge_next, edge_last = lead(info, vec_ids, pool, winds)
    before_edge = lax.ppermute(edge_next, ALL, FORWARD)
    after_edge = lax.ppermute(edge_last, ALL, BACKWARD)
    low, high, wind, next_0, next_1, last_0, last_1, basis_main, basis_rest = pack(
        info, vec_ids, pool, winds, basis
    )
    to_east, to_west, *bulk = edges(
        (before_edge, after_edge, low, high, wind), (next_0, last_0, next_1, last_1)
    )
    west = lax.ppermute(to_east, "lon", EASTWARD)
    east = lax.ppermute(to_west, "lon", WESTWARD)
    before_0, after_0 = lax.ppermute(bulk[0], ALL, FORWARD), lax.ppermute(bulk[1], ALL, BACKWARD)
    before_1, after_1 = lax.ppermute(bulk[2], ALL, FORWARD), lax.ppermute(bulk[3], ALL, BACKWARD)
    levels = jnp.asarray(np.arange(CH, dtype=np.int32)[None] % LEV)
    wind_ext, spread = frame_winds(info, before_edge, after_edge, wind, west, east, levels)

    level_mix = jnp.concatenate(
        [mixing.reshape(TR, LEV - 1), jnp.zeros((TR, 1), mixing.dtype)], axis=1
    )
    upper = jnp.tile(level_mix.reshape(GROUP), VEC)
    mix = jnp.stack([upper, jnp.roll(upper, 1)])
    rows = (jnp.arange(ROWS, dtype=jnp.int32) + lat_index * ROWS).astype(jnp.float32)
    cosine = jnp.cos((rows + 0.5) * (math.pi / (ROWS * 8)) - math.pi / 2)
    scalars = (info, wind_ids, cosine)
    tile = (before_edge, low, high, after_edge, west, east)
    arrays = (levels, mix, basis_main, basis_rest, before_0, after_0)
    half, mine, theirs = window(0, scalars, (*tile, wind_ext, *arrays))
    first = mine + lax.ppermute(theirs, ALL, moved(dc=1))
    sensitivity, mine, theirs = window(
        1, scalars, (*tile, spread, *arrays, before_1, after_1, half)
    )
    second = mine + lax.ppermute(theirs, ALL, moved(dc=1))

    first = line_sum(first.reshape(4, 8, BLOCK, 128), dz=1)
    second = line_sum(second.reshape(4, 8, BLOCK, 128), dx=1)
    first = line_sum(first.reshape(4, 2, BLOCK, 128), dx=1)
    second = line_sum(second.reshape(4, 2, BLOCK, 128), dz=1)
    near = jnp.where(flip == 0, first, second)
    far = jnp.where(flip == 0, second, first)
    block = near[0] + lax.ppermute(near[1], ALL, turned(1))
    block += lax.ppermute(far[0], ALL, turned(2)) + lax.ppermute(far[1], ALL, turned(3))
    ritz = jnp.concatenate([block[:LEV].T, block[LEV:, :LEV]], axis=0)
    return sensitivity, ritz * (1.0 / math.sqrt(ROWS * COLS * 128))


def solution(mesh):
    in_specs = (P("lat", "lon", None), P(), P("lat", "lon", None), P(), P(), P("lat", "lon", None))
    out_specs = (P("lat", "lon", None), P("lat", "lon"))
    return jax.shard_map(shards, mesh=mesh, in_specs=in_specs, out_specs=out_specs, check_vma=False)
```

```python
import functools
import functools
import math

import jax
import jax.numpy as jnp
import numpy as np
from jax import lax
from jax.experimental import pallas as pl
from jax.experimental.pallas import tpu as pltpu
from jax.sharding import PartitionSpec as P

LEV = 72
TR = 2
VEC = 8
POOL = 8
NSLAB = 2
STEPS = 4
DIFFUSE = 0.075
ALL = ("lat", "lon")

ROWS = 8
COLS = 48
CH = VEC * TR * LEV
GROUP = TR * LEV
WCH = NSLAB * 2 * LEV
D = STEPS
EXT = ROWS + 2 * D
PITCH = 80
FIRST = 16
SPAN = 64
WPACK = 896
PART = 640
BLOCK = 88


def place(x, y, z, core):
    return (x * 2 + y % 2) * 16 + (y // 2) * 8 + z * 2 + core


PLACES = [(x, y, z, c) for x in range(4) for y in range(4) for z in range(4) for c in range(2)]


def moved(dx=0, dy=0, dz=0, dc=0):
    return [
        (place(x, y, z, c), place((x + dx) % 4, (y + dy) % 4, (z + dz) % 4, c ^ dc))
        for x, y, z, c in PLACES
    ]


def turned(bits):
    return [(place(x, y, z, c), place(x, y ^ bits, z, c)) for x, y, z, c in PLACES]


def meridian():
    pairs = []
    for b in range(8):
        for a in range(8):
            pairs.append((a * 16 + b, (a + 1) * 16 + b if a < 7 else a * 16 + b + 8))
            pairs.append((a * 16 + b + 8, (a - 1) * 16 + b + 8 if a > 0 else a * 16 + b))
    return pairs


FORWARD = meridian()
BACKWARD = [(t, s) for s, t in FORWARD]
EASTWARD = [(b, (b + 1) % 16) for b in range(16)]
WESTWARD = [(t, s) for s, t in EASTWARD]


def edge_tile(r, m):
    i = r * (CH // 128) + m
    return slice(i // 6 * 8, i // 6 * 8 + 8), slice(WPACK + i % 6 * 128, WPACK + i % 6 * 128 + 128)


def choose(vec_ids, chosen):
    lane = lax.broadcasted_iota(jnp.int32, (1, CH), 1)
    source = lane
    for k in range(VEC):
        inside = (lane >= k * GROUP) & (lane < (k + 1) * GROUP)
        source = jnp.where(inside, lane + (vec_ids[k] - k) * GROUP, source)
    for i in range(CH // 128):
        row = lax.broadcasted_iota(jnp.int32, (128, CH), 0) + i * 128
        chosen[i * 128 : (i + 1) * 128, :] = jnp.where(row == source, 1.0, 0.0).astype(jnp.bfloat16)


def turned_wind(winds, info, r):
    place_in_slab = lax.rem(lax.broadcasted_iota(jnp.int32, (1, WCH), 1), 2 * LEV)
    turn = jnp.where((place_in_slab >= LEV) & (info[0] != 0), -1.0, 1.0)
    return winds[jnp.where(info[0] == 0, r, ROWS - 1 - r)] * turn


def lead_kernel(
    info, vec_ids, pool, winds, edge_next, edge_last, chosen, ends, held_winds, made, sems
):
    fetch = [
        pltpu.make_async_copy(pool.at[:, :16, :], ends.at[0], sems.at[0]),
        pltpu.make_async_copy(pool.at[:, COLS - 16 :, :], ends.at[1], sems.at[1]),
        pltpu.make_async_copy(winds, held_winds, sems.at[2]),
    ]
    for copy in fetch:
        copy.start()
    choose(vec_ids, chosen)
    for copy in fetch:
        copy.wait()
    for i in range(2):
        rows = ends[i].reshape(ROWS * 16, CH)
        picked = jnp.dot(rows, chosen[...], preferred_element_type=jnp.float32)
        made[i] = picked.reshape(ROWS, 16, CH)
    for r in range(4):
        for edge, row in ((edge_last, r), (edge_next, 4 + r)):
            own = jnp.where(info[0] == 0, row, ROWS - 1 - row)
            for m in range(CH // 128):
                lanes = slice(m * 128, (m + 1) * 128)
                where = edge_tile(r, m)
                edge[where[0], where[1]] = jnp.concatenate(
                    [made[0, own, :4, lanes], made[1, own, 12:, lanes]], axis=0
                )
    for r in range(3):
        lanes = slice(r * WCH, (r + 1) * WCH)
        edge_last[:, lanes] = turned_wind(held_winds, info, r)
        edge_next[:, lanes] = turned_wind(held_winds, info, ROWS - 3 + r)


def lead(info, vec_ids, pool, winds):
    vmem = pl.BlockSpec(memory_space=pltpu.VMEM)
    return pl.pallas_call(
        lead_kernel,
        out_shape=[jax.ShapeDtypeStruct((COLS, WPACK + 768), jnp.float32)] * 2,
        in_specs=[pl.BlockSpec(memory_space=pltpu.SMEM)] * 2
        + [pl.BlockSpec(memory_space=pltpu.HBM)] * 2,
        out_specs=[vmem] * 2,
        scratch_shapes=[
            pltpu.VMEM((CH, CH), jnp.bfloat16),
            pltpu.VMEM((2, ROWS, 16, CH), jnp.bfloat16),
            pltpu.VMEM((ROWS, COLS, WCH), jnp.float32),
            pltpu.VMEM((2, ROWS, 16, CH), jnp.float32),
            pltpu.SemaphoreType.DMA((3,)),
        ],
        compiler_params=pltpu.CompilerParams(vmem_limit_bytes=60 << 20),
        cost_estimate=pl.CostEstimate(flops=1 << 30, bytes_accessed=4 << 20, transcendentals=0),
        name="lead",
    )(info, vec_ids, pool, winds)


def pack_kernel(
    info, vec_ids, pool, winds, basis,
    low, high, wind, next_0, next_1, last_0, last_1, basis_main, basis_rest, chosen,
):
    choose(vec_ids, chosen)
    for half in range(2):
        rows = pool[half * 4 : half * 4 + 4].reshape(4 * COLS, CH)
        picked = jnp.dot(rows, chosen[...], preferred_element_type=jnp.float32)
        picked = picked.reshape(4, COLS, CH)

        @pl.when(info[0] == 0)
        def _():
            (low, high)[half][...] = picked

        @pl.when(info[0] != 0)
        def _():
            for r in range(4):
                (high, low)[half][3 - r] = picked[r]

    for rows, bulk_0, bulk_1 in ((high, next_0, next_1), (low, last_0, last_1)):
        for r in range(4):
            bulk_0[r] = rows[r, 4 : COLS - 4, :PART]
            bulk_1[r] = rows[r, 4 : COLS - 4, PART:]
    for r in range(ROWS):
        wind[r] = turned_wind(winds, info, r)
    flat = basis[...].reshape(ROWS * COLS, CH)
    for a in range(8):
        basis_main[:, a * 128 : (a + 1) * 128] = flat[:, a * 144 : a * 144 + 128]
        basis_rest[:, a * 16 : (a + 1) * 16] = flat[:, a * 144 + 128 : (a + 1) * 144]


def pack(info, vec_ids, pool, winds, basis):
    shapes = [(4, COLS, CH)] * 2 + [(ROWS, COLS, WCH)]
    shapes += [(4, COLS - 8, PART), (4, COLS - 8, CH - PART)] * 2
    outs = [jax.ShapeDtypeStruct(s, jnp.float32) for s in shapes]
    outs += [jax.ShapeDtypeStruct((ROWS * COLS, n), jnp.bfloat16) for n in (1024, 128)]
    vmem = pl.BlockSpec(memory_space=pltpu.VMEM)
    return pl.pallas_call(
        pack_kernel,
        out_shape=outs,
        in_specs=[pl.BlockSpec(memory_space=pltpu.SMEM)] * 2 + [vmem] * 3,
        out_specs=[vmem] * 9,
        scratch_shapes=[pltpu.VMEM((CH, CH), jnp.bfloat16)],
        compiler_params=pltpu.CompilerParams(vmem_limit_bytes=24 << 20),
        cost_estimate=pl.CostEstimate(flops=1 << 30, bytes_accessed=4 << 20, transcendentals=0),
        name="pack",
    )(info, vec_ids, pool, winds, basis)


SIDE = EXT - 2


def edges_kernel(before, after, low, high, wind, *rest):
    to_east, to_west = rest[4:6]
    for first, near, target in ((COLS - 4, 4, to_east), (0, 0, to_west)):
        columns = slice(first, first + 4)
        for r in range(3):
            for m in range(CH // 128):
                lanes = slice(m * 128, (m + 1) * 128)
                where = edge_tile(r + 1, m)
                target[r, :, lanes] = before[where[0], where[1]][near : near + 4]
                where = edge_tile(r, m)
                target[11 + r, :, lanes] = after[where[0], where[1]][near : near + 4]
        for r in range(4):
            target[3 + r] = low[r, columns, :]
            target[7 + r] = high[r, columns, :]
        for r in range(SIDE):
            if r < 3:
                line = before[columns, r * WCH : (r + 1) * WCH]
            elif r < 11:
                line = wind[r - 3, columns, :]
            else:
                line = after[columns, (r - 11) * WCH : (r - 10) * WCH]
            target[SIDE + r // 4, :, r % 4 * WCH : (r % 4 + 1) * WCH] = line


def edges(arrays, bulk):
    vmem = pl.BlockSpec(memory_space=pltpu.VMEM)
    anywhere = pl.BlockSpec(memory_space=pl.ANY)
    shapes = [jax.ShapeDtypeStruct((SIDE + 4, 4, CH), jnp.float32)] * 2
    return pl.pallas_call(
        edges_kernel,
        out_shape=shapes + [jax.ShapeDtypeStruct(b.shape, b.dtype) for b in bulk],
        in_specs=[vmem] * 5 + [anywhere] * 4,
        out_specs=[vmem] * 2 + [anywhere] * 4,
        input_output_aliases={5 + i: 2 + i for i in range(4)},
        compiler_params=pltpu.CompilerParams(vmem_limit_bytes=16 << 20),
        cost_estimate=pl.CostEstimate(flops=1 << 20, bytes_accessed=4 << 20, transcendentals=0),
        name="edges",
    )(*arrays, *bulk)


def repeat_winds(wind_ext, levels, lanes, spread):
    level = lax.broadcasted_iota(jnp.int32, (2 * LEV, PART), 0)
    level = jnp.where(level >= LEV, level - LEV, level)
    repeat = jnp.where(level == levels[:, lanes], 1.0, 0.0).astype(jnp.bfloat16)
    flat = wind_ext[...].reshape(SIDE * SPAN, WCH)
    for i in range(2 * NSLAB):
        value = flat[:, i * LEV : (i + 1) * LEV]
        coarse = value.astype(jnp.bfloat16)
        fine = (value - coarse.astype(jnp.float32)).astype(jnp.bfloat16)
        both = jnp.concatenate([coarse, fine], axis=1)
        spread[i] = jnp.dot(both, repeat, preferred_element_type=jnp.float32).reshape(
            SIDE, SPAN, PART
        )


def frame_kernel(info, before, after, wind, west, east, levels, wind_ext, spread):
    turn_west, turn_east = info[5], info[6]
    for r in range(3):
        lanes = slice(r * WCH, (r + 1) * WCH)
        wind_ext[r, 8 : 8 + COLS] = before[:, lanes]
        wind_ext[11 + r, 8 : 8 + COLS] = after[:, lanes]
    for r in range(ROWS):
        wind_ext[3 + r, 8 : 8 + COLS] = wind[r]
    lane = lax.rem(lax.broadcasted_iota(jnp.int32, (1, WCH), 1), 2 * LEV)
    for turn, payload, first in ((turn_west, west, 4), (turn_east, east, 8 + COLS)):
        sign = jnp.where((lane >= LEV) & (turn != 0), -1.0, 1.0)
        for r in range(SIDE):
            line = payload[SIDE + r // 4, :, r % 4 * WCH : (r % 4 + 1) * WCH] * sign
            wind_ext[jnp.where(turn == 0, r, SIDE - 1 - r), first : first + 4] = line
    repeat_winds(wind_ext, levels, slice(512, 512 + PART), spread)


def frame_winds(info, *arrays):
    vmem = pl.BlockSpec(memory_space=pltpu.VMEM)
    return pl.pallas_call(
        frame_kernel,
        out_shape=[
            jax.ShapeDtypeStruct((SIDE, SPAN, WCH), jnp.float32),
            jax.ShapeDtypeStruct((2 * NSLAB, SIDE, SPAN, PART), jnp.float32),
        ],
        in_specs=[pl.BlockSpec(memory_space=pltpu.SMEM)] + [vmem] * 6,
        out_specs=[vmem] * 2,
        compiler_params=pltpu.CompilerParams(vmem_limit_bytes=24 << 20),
        cost_estimate=pl.CostEstimate(flops=16 << 30, bytes_accessed=4 << 20, transcendentals=0),
        name="frame",
    )(info, *arrays)


def window_kernel(
    part, info, wind_ids, cosine,
    before_edge, low, high, after_edge, west, east, wind_ext,
    levels, mix, basis_main, basis_rest, before_0, after_0,
    *others,
):
    before_1, after_1, earlier = others[:3] if part else (None, None, None)
    out, mine, theirs, state_a, state_b, weighted, gram, rest, *spread = others[3 * part :]
    spread = spread[0] if spread else None
    flip, mx, my, mz, mc, turn_west, turn_east = (info[i] for i in range(7))
    lanes = slice(part * 512, part * 512 + PART)
    skip = part * 64

    for r in range(4):
        state_a[4 + r, FIRST : FIRST + COLS] = low[r, :, lanes]
        state_a[8 + r, FIRST : FIRST + COLS] = high[r, :, lanes]
        for row, edge, bulk_0, bulk_1 in (
            (r, before_edge, before_0, before_1),
            (12 + r, after_edge, after_0, after_1),
        ):
            middle = slice(FIRST + 4, FIRST + COLS - 4)
            if part:
                state_a[row, middle, :128] = bulk_0[r, :, 512:]
                state_a[row, middle, 128:] = bulk_1[r]
            else:
                state_a[row, middle] = bulk_0[r]
            for m in range(PART // 128):
                tile = slice(m * 128, (m + 1) * 128)
                where = edge_tile(r, m + part * 4)
                ends = edge[where[0], where[1]]
                state_a[row, FIRST : FIRST + 4, tile] = ends[:4]
                state_a[row, FIRST + COLS - 4 : FIRST + COLS, tile] = ends[4:]
    for r in range(SIDE):
        from_west = jnp.where(turn_west == 0, r, SIDE - 1 - r)
        from_east = jnp.where(turn_east == 0, r, SIDE - 1 - r)
        state_a[1 + r, FIRST - 4 : FIRST] = west[from_west, :, lanes]
        state_a[1 + r, FIRST + COLS : FIRST + COLS + 4] = east[from_east, :, lanes]

    if part:
        spread = wind_ext
    else:
        repeat_winds(wind_ext, levels, lanes, spread)

    up, down = mix[0:1, lanes], mix[1:2, lanes]

    def updated(source, slab, r, c):
        now = source[r, pl.ds(c, 8), :]
        after = source[r + 1, pl.ds(c, 8), :]
        before = source[r - 1, pl.ds(c, 8), :]
        east_side = source[r, pl.ds(c + 1, 8), :]
        west_side = source[r, pl.ds(c - 1, 8), :]
        u = spread[2 * slab, r - 1, pl.ds(c - FIRST + 8, 8), :]
        v = spread[2 * slab + 1, r - 1, pl.ds(c - FIRST + 8, 8), :]
        gain_east = jnp.maximum(u, 0.0) + DIFFUSE
        gain_after = jnp.maximum(v, 0.0) + DIFFUSE
        change = gain_east * (east_side - now) + (gain_east - u) * (west_side - now)
        change += gain_after * (after - now) + (gain_after - v) * (before - now)
        above, below = pltpu.roll(now, PART - 1, 1), pltpu.roll(now, 1, 1)
        change += up * (above - now) - down * (now - below)
        return now + change

    buffers = (state_a, state_b)
    for step in range(STEPS - 1):
        source, target = buffers[step % 2], buffers[(step + 1) % 2]
        slab = wind_ids[step]

        def body(r, carry):
            for c in range(FIRST - 8, FIRST - 8 + SPAN, 8):
                target[r, c : c + 8, :] = updated(source, slab, r, c)
            return carry

        lax.fori_loop(1 + step, EXT - 1 - step, body, 0)

    source = buffers[(STEPS - 1) % 2]
    slab = wind_ids[STEPS - 1]
    own_lanes = lax.broadcasted_iota(jnp.int32, (16, 128), 1) >= skip

    def last(r, carry):
        own = jnp.where(flip == 0, r - D, ROWS - 1 - (r - D))
        share = cosine[own]
        for c in range(0, COLS, 16):
            first = updated(source, slab, r, FIRST + c)
            second = updated(source, slab, r, FIRST + c + 8)
            both = jnp.concatenate([first, second], axis=0)
            if part:
                there = slice(c, c + 16)
                out[own, there, :512] = earlier[own, there, :512]
                out[own, there, 512:640] = jnp.where(
                    own_lanes, both[:, :128], earlier[own, there, 512:]
                )
                out[own, there, 640:] = both[:, 128:]
            else:
                out[own, c : c + 16, :] = both
            weighted[own, c : c + 16, :] = (both * share).astype(jnp.bfloat16)
        return carry

    lax.fori_loop(D, D + ROWS, last, 0)

    flat_weighted = weighted[...].reshape(ROWS * COLS, PART)
    across = (((0,), (0,)), ((), ()))
    for i in range(PART // 128):
        gram[i * 128 : (i + 1) * 128, :] = lax.dot_general(
            flat_weighted[:, i * 128 : (i + 1) * 128],
            basis_main[...],
            across,
            preferred_element_type=jnp.float32,
        )
    tail = lax.dot_general(
        basis_rest[...], flat_weighted, across, preferred_element_type=jnp.float32
    )
    for g in range(8):
        rest[g, :, :LEV] = tail[:, skip + g * LEV : skip + (g + 1) * LEV]

    def place_blocks(i, carry):
        rz, rx, ry = i // 8, (i // 2) % 4, i % 2
        z, x = (mz + rz) % 4, (mx + rx) % 4
        outer, inner = (rx, rz) if part else (rz, rx)
        at = outer * 8 + inner * 2 + ry
        a = x * 2 + (my ^ ry)
        for dc, target in ((0, mine), (1, theirs)):
            g = z * 2 + (mc ^ dc)
            target[at, :LEV] = gram[
                pl.ds(pl.multiple_of(skip + g * LEV, 8), LEV),
                pl.ds(pl.multiple_of(a * 128, 128), 128),
            ]
            target[at, LEV:] = rest[g, pl.ds(pl.multiple_of(a * 16, 16), 16), :]
        return carry

    lax.fori_loop(0, 32, place_blocks, 0, unroll=8)


def window(part, scalars, arrays):
    blocks = jax.ShapeDtypeStruct((32, BLOCK, 128), jnp.float32)
    vmem = pl.BlockSpec(memory_space=pltpu.VMEM)
    return pl.pallas_call(
        functools.partial(window_kernel, part),
        out_shape=[
            jax.ShapeDtypeStruct((ROWS, COLS, CH if part else PART), jnp.float32),
            blocks,
            blocks,
        ],
        in_specs=[pl.BlockSpec(memory_space=pltpu.SMEM)] * len(scalars) + [vmem] * len(arrays),
        out_specs=[vmem] * 3,
        scratch_shapes=[
            pltpu.VMEM((EXT, PITCH, PART), jnp.float32),
            pltpu.VMEM((EXT, PITCH, PART), jnp.float32),
            pltpu.VMEM((ROWS, COLS, PART), jnp.bfloat16),
            pltpu.VMEM((PART, 1024), jnp.float32),
            pltpu.VMEM((8, 128, 128), jnp.float32),
        ]
        + [pltpu.VMEM((2 * NSLAB, SIDE, SPAN, PART), jnp.float32)] * (1 - part),
        compiler_params=pltpu.CompilerParams(vmem_limit_bytes=(24 if part else 32) << 20),
        cost_estimate=pl.CostEstimate(flops=8 << 30, bytes_accessed=16 << 20, transcendentals=0),
        name=f"window_{part}",
    )(*scalars, *arrays)


def line_sum(parts, **axis):
    (name,) = axis
    sent = [lax.ppermute(parts[k], ALL, moved(**{name: k})) for k in (1, 2, 3)]
    return (parts[0] + sent[0]) + (sent[1] + sent[2])


def ring_sum(parts, **axis):
    (name,) = axis
    up, down = moved(**{name: 1}), moved(**{name: -1})
    from_below = lax.ppermute(parts[3:5], ALL, up)
    from_above = lax.ppermute(parts[5:7], ALL, down)
    last_below = lax.ppermute(parts[2] + from_below[1], ALL, up)
    last_above = lax.ppermute(parts[7] + from_above[0], ALL, down)
    return jnp.stack(
        [parts[0] + from_above[1] + last_below, parts[1] + from_below[0] + last_above]
    )


def shards(pool, vec_ids, winds, wind_ids, mixing, basis):
    lat_index = lax.axis_index("lat").astype(jnp.int32)
    lon_index = lax.axis_index("lon").astype(jnp.int32)
    flip = lon_index // 8
    info = jnp.stack(
        [
            flip,
            lat_index // 2,
            lat_index % 2,
            (lon_index // 2) % 4,
            lon_index % 2,
            (lon_index % 8 == 0).astype(jnp.int32),
            (lon_index % 8 == 7).astype(jnp.int32),
        ]
    )
    edge_next, edge_last = lead(info, vec_ids, pool, winds)
    before_edge = lax.ppermute(edge_next, ALL, FORWARD)
    after_edge = lax.ppermute(edge_last, ALL, BACKWARD)
    low, high, wind, next_0, next_1, last_0, last_1, basis_main, basis_rest = pack(
        info, vec_ids, pool, winds, basis
    )
    to_east, to_west, *bulk = edges(
        (before_edge, after_edge, low, high, wind), (next_0, last_0, next_1, last_1)
    )
    west = lax.ppermute(to_east, "lon", EASTWARD)
    east = lax.ppermute(to_west, "lon", WESTWARD)
    before_0, after_0 = lax.ppermute(bulk[0], ALL, FORWARD), lax.ppermute(bulk[1], ALL, BACKWARD)
    before_1, after_1 = lax.ppermute(bulk[2], ALL, FORWARD), lax.ppermute(bulk[3], ALL, BACKWARD)
    levels = jnp.asarray(np.arange(CH, dtype=np.int32)[None] % LEV)
    wind_ext, spread = frame_winds(info, before_edge, after_edge, wind, west, east, levels)

    level_mix = jnp.concatenate(
        [mixing.reshape(TR, LEV - 1), jnp.zeros((TR, 1), mixing.dtype)], axis=1
    )
    upper = jnp.tile(level_mix.reshape(GROUP), VEC)
    mix = jnp.stack([upper, jnp.roll(upper, 1)])
    rows = (jnp.arange(ROWS, dtype=jnp.int32) + lat_index * ROWS).astype(jnp.float32)
    cosine = jnp.cos((rows + 0.5) * (math.pi / (ROWS * 8)) - math.pi / 2)
    scalars = (info, wind_ids, cosine)
    tile = (before_edge, low, high, after_edge, west, east)
    arrays = (levels, mix, basis_main, basis_rest, before_0, after_0)
    half, mine, theirs = window(0, scalars, (*tile, wind_ext, *arrays))
    first = mine + lax.ppermute(theirs, ALL, moved(dc=1))
    sensitivity, mine, theirs = window(
        1, scalars, (*tile, spread, *arrays, before_1, after_1, half)
    )
    second = mine + lax.ppermute(theirs, ALL, moved(dc=1))

    first = ring_sum(first.reshape(8, 4, BLOCK, 128), dz=1)
    second = line_sum(second.reshape(4, 8, BLOCK, 128), dx=1)
    first = line_sum(first.reshape(4, 2, BLOCK, 128), dx=1)
    second = line_sum(second.reshape(4, 2, BLOCK, 128), dz=1)
    near = jnp.where(flip == 0, first, second)
    far = jnp.where(flip == 0, second, first)
    block = near[0] + lax.ppermute(near[1], ALL, turned(1))
    block += lax.ppermute(far[0], ALL, turned(2)) + lax.ppermute(far[1], ALL, turned(3))
    ritz = jnp.concatenate([block[:LEV].T, block[LEV:, :LEV]], axis=0)
    return sensitivity, ritz * (1.0 / math.sqrt(ROWS * COLS * 128))


def solution(mesh):
    in_specs = (P("lat", "lon", None), P(), P("lat", "lon", None), P(), P(), P("lat", "lon", None))
    out_specs = (P("lat", "lon", None), P("lat", "lon"))
    return jax.shard_map(shards, mesh=mesh, in_specs=in_specs, out_specs=out_specs, check_vma=False)
```

```python
import functools
import functools
import math

import jax
import jax.numpy as jnp
import numpy as np
from jax import lax
from jax.experimental import pallas as pl
from jax.experimental.pallas import tpu as pltpu
from jax.sharding import PartitionSpec as P

LEV = 72
TR = 2
VEC = 8
POOL = 8
NSLAB = 2
STEPS = 4
DIFFUSE = 0.075
ALL = ("lat", "lon")

ROWS = 8
COLS = 48
CH = VEC * TR * LEV
GROUP = TR * LEV
WCH = NSLAB * 2 * LEV
D = STEPS
EXT = ROWS + 2 * D
PITCH = 80
FIRST = 16
SPAN = 64
WPACK = 896
PART = 640
BLOCK = 88


def place(x, y, z, core):
    return (x * 2 + y % 2) * 16 + (y // 2) * 8 + z * 2 + core


PLACES = [(x, y, z, c) for x in range(4) for y in range(4) for z in range(4) for c in range(2)]


def moved(dx=0, dy=0, dz=0, dc=0):
    return [
        (place(x, y, z, c), place((x + dx) % 4, (y + dy) % 4, (z + dz) % 4, c ^ dc))
        for x, y, z, c in PLACES
    ]


def turned(bits):
    return [(place(x, y, z, c), place(x, y ^ bits, z, c)) for x, y, z, c in PLACES]


def meridian():
    pairs = []
    for b in range(8):
        for a in range(8):
            pairs.append((a * 16 + b, (a + 1) * 16 + b if a < 7 else a * 16 + b + 8))
            pairs.append((a * 16 + b + 8, (a - 1) * 16 + b + 8 if a > 0 else a * 16 + b))
    return pairs


FORWARD = meridian()
CIRCLE = FORWARD + [(t, s) for s, t in FORWARD]
SWAP_A = [(s, t) for s, t in CIRCLE if s // 16 // 2 == t // 16 // 2 and s // 16 != t // 16]
SWAP_B = [pair for pair in CIRCLE if pair not in SWAP_A]
EASTWARD = [(b, (b + 1) % 16) for b in range(16)]
WESTWARD = [(t, s) for s, t in EASTWARD]


def edge_tile(r, m):
    i = r * (CH // 128) + m
    return slice(i // 6 * 8, i // 6 * 8 + 8), slice(WPACK + i % 6 * 128, WPACK + i % 6 * 128 + 128)


def choose(vec_ids, chosen):
    lane = lax.broadcasted_iota(jnp.int32, (1, CH), 1)
    source = lane
    for k in range(VEC):
        inside = (lane >= k * GROUP) & (lane < (k + 1) * GROUP)
        source = jnp.where(inside, lane + (vec_ids[k] - k) * GROUP, source)
    for i in range(CH // 128):
        row = lax.broadcasted_iota(jnp.int32, (128, CH), 0) + i * 128
        chosen[i * 128 : (i + 1) * 128, :] = jnp.where(row == source, 1.0, 0.0).astype(jnp.bfloat16)


def turned_wind(winds, info, r):
    place_in_slab = lax.rem(lax.broadcasted_iota(jnp.int32, (1, WCH), 1), 2 * LEV)
    turn = jnp.where((place_in_slab >= LEV) & (info[0] != 0), -1.0, 1.0)
    return winds[jnp.where(info[0] == 0, r, ROWS - 1 - r)] * turn


def lead_kernel(
    info, vec_ids, pool, winds, edge_a, edge_b, chosen, ends, held_winds, made, sems
):
    fetch = [
        pltpu.make_async_copy(pool.at[:, :16, :], ends.at[0], sems.at[0]),
        pltpu.make_async_copy(pool.at[:, COLS - 16 :, :], ends.at[1], sems.at[1]),
        pltpu.make_async_copy(winds, held_winds, sems.at[2]),
    ]
    for copy in fetch:
        copy.start()
    choose(vec_ids, chosen)
    for copy in fetch:
        copy.wait()
    for i in range(2):
        rows = ends[i].reshape(ROWS * 16, CH)
        picked = jnp.dot(rows, chosen[...], preferred_element_type=jnp.float32)
        made[i] = picked.reshape(ROWS, 16, CH)
    for r in range(4):
        for edge, flag in ((edge_a, info[7]), (edge_b, 1 - info[7])):
            row = jnp.where(flag == 0, 4 + r, r)
            own = jnp.where(info[0] == 0, row, ROWS - 1 - row)
            for m in range(CH // 128):
                lanes = slice(m * 128, (m + 1) * 128)
                where = edge_tile(r, m)
                edge[where[0], where[1]] = jnp.concatenate(
                    [made[0, own, :4, lanes], made[1, own, 12:, lanes]], axis=0
                )
    for r in range(3):
        lanes = slice(r * WCH, (r + 1) * WCH)
        for edge, flag in ((edge_a, info[7]), (edge_b, 1 - info[7])):
            row = jnp.where(flag == 0, ROWS - 3 + r, r)
            edge[:, lanes] = turned_wind(held_winds, info, row)


def lead(info, vec_ids, pool, winds):
    vmem = pl.BlockSpec(memory_space=pltpu.VMEM)
    return pl.pallas_call(
        lead_kernel,
        out_shape=[jax.ShapeDtypeStruct((COLS, WPACK + 768), jnp.float32)] * 2,
        in_specs=[pl.BlockSpec(memory_space=pltpu.SMEM)] * 2
        + [pl.BlockSpec(memory_space=pltpu.HBM)] * 2,
        out_specs=[vmem] * 2,
        scratch_shapes=[
            pltpu.VMEM((CH, CH), jnp.bfloat16),
            pltpu.VMEM((2, ROWS, 16, CH), jnp.bfloat16),
            pltpu.VMEM((ROWS, COLS, WCH), jnp.float32),
            pltpu.VMEM((2, ROWS, 16, CH), jnp.float32),
            pltpu.SemaphoreType.DMA((3,)),
        ],
        compiler_params=pltpu.CompilerParams(vmem_limit_bytes=60 << 20),
        cost_estimate=pl.CostEstimate(flops=1 << 30, bytes_accessed=4 << 20, transcendentals=0),
        name="lead",
    )(info, vec_ids, pool, winds)


def pack_kernel(
    info, vec_ids, pool, winds, basis,
    low, high, wind, a_0, a_1, b_0, b_1, basis_main, basis_rest, chosen,
):
    choose(vec_ids, chosen)
    for half in range(2):
        rows = pool[half * 4 : half * 4 + 4].reshape(4 * COLS, CH)
        picked = jnp.dot(rows, chosen[...], preferred_element_type=jnp.float32)
        picked = picked.reshape(4, COLS, CH)

        @pl.when(info[0] == 0)
        def _():
            (low, high)[half][...] = picked

        @pl.when(info[0] != 0)
        def _():
            for r in range(4):
                (high, low)[half][3 - r] = picked[r]

    for flag, bulk_0, bulk_1 in ((info[7], a_0, a_1), (1 - info[7], b_0, b_1)):
        for r in range(4):
            line = jnp.where(flag == 0, high[r, 4 : COLS - 4, :], low[r, 4 : COLS - 4, :])
            bulk_0[r] = line[:, :PART]
            bulk_1[r] = line[:, PART:]
    for r in range(ROWS):
        wind[r] = turned_wind(winds, info, r)
    flat = basis[...].reshape(ROWS * COLS, CH)
    for a in range(8):
        basis_main[:, a * 128 : (a + 1) * 128] = flat[:, a * 144 : a * 144 + 128]
        basis_rest[:, a * 16 : (a + 1) * 16] = flat[:, a * 144 + 128 : (a + 1) * 144]


def pack(info, vec_ids, pool, winds, basis):
    shapes = [(4, COLS, CH)] * 2 + [(ROWS, COLS, WCH)]
    shapes += [(4, COLS - 8, PART), (4, COLS - 8, CH - PART)] * 2
    outs = [jax.ShapeDtypeStruct(s, jnp.float32) for s in shapes]
    outs += [jax.ShapeDtypeStruct((ROWS * COLS, n), jnp.bfloat16) for n in (1024, 128)]
    vmem = pl.BlockSpec(memory_space=pltpu.VMEM)
    return pl.pallas_call(
        pack_kernel,
        out_shape=outs,
        in_specs=[pl.BlockSpec(memory_space=pltpu.SMEM)] * 2 + [vmem] * 3,
        out_specs=[vmem] * 9,
        scratch_shapes=[pltpu.VMEM((CH, CH), jnp.bfloat16)],
        compiler_params=pltpu.CompilerParams(vmem_limit_bytes=24 << 20),
        cost_estimate=pl.CostEstimate(flops=1 << 30, bytes_accessed=4 << 20, transcendentals=0),
        name="pack",
    )(info, vec_ids, pool, winds, basis)


SIDE = EXT - 2


def edges_kernel(before, after, low, high, wind, *rest):
    to_east, to_west = rest[4:6]
    for first, near, target in ((COLS - 4, 4, to_east), (0, 0, to_west)):
        columns = slice(first, first + 4)
        for r in range(3):
            for m in range(CH // 128):
                lanes = slice(m * 128, (m + 1) * 128)
                where = edge_tile(r + 1, m)
                target[r, :, lanes] = before[where[0], where[1]][near : near + 4]
                where = edge_tile(r, m)
                target[11 + r, :, lanes] = after[where[0], where[1]][near : near + 4]
        for r in range(4):
            target[3 + r] = low[r, columns, :]
            target[7 + r] = high[r, columns, :]
        for r in range(SIDE):
            if r < 3:
                line = before[columns, r * WCH : (r + 1) * WCH]
            elif r < 11:
                line = wind[r - 3, columns, :]
            else:
                line = after[columns, (r - 11) * WCH : (r - 10) * WCH]
            target[SIDE + r // 4, :, r % 4 * WCH : (r % 4 + 1) * WCH] = line


def edges(arrays, bulk):
    vmem = pl.BlockSpec(memory_space=pltpu.VMEM)
    anywhere = pl.BlockSpec(memory_space=pl.ANY)
    shapes = [jax.ShapeDtypeStruct((SIDE + 4, 4, CH), jnp.float32)] * 2
    return pl.pallas_call(
        edges_kernel,
        out_shape=shapes + [jax.ShapeDtypeStruct(b.shape, b.dtype) for b in bulk],
        in_specs=[vmem] * 5 + [anywhere] * 4,
        out_specs=[vmem] * 2 + [anywhere] * 4,
        input_output_aliases={5 + i: 2 + i for i in range(4)},
        compiler_params=pltpu.CompilerParams(vmem_limit_bytes=16 << 20),
        cost_estimate=pl.CostEstimate(flops=1 << 20, bytes_accessed=4 << 20, transcendentals=0),
        name="edges",
    )(*arrays, *bulk)


def repeat_winds(wind_ext, levels, lanes, spread):
    level = lax.broadcasted_iota(jnp.int32, (2 * LEV, PART), 0)
    level = jnp.where(level >= LEV, level - LEV, level)
    repeat = jnp.where(level == levels[:, lanes], 1.0, 0.0).astype(jnp.bfloat16)
    flat = wind_ext[...].reshape(SIDE * SPAN, WCH)
    for i in range(2 * NSLAB):
        value = flat[:, i * LEV : (i + 1) * LEV]
        coarse = value.astype(jnp.bfloat16)
        fine = (value - coarse.astype(jnp.float32)).astype(jnp.bfloat16)
        both = jnp.concatenate([coarse, fine], axis=1)
        spread[i] = jnp.dot(both, repeat, preferred_element_type=jnp.float32).reshape(
            SIDE, SPAN, PART
        )


def frame_kernel(info, before, after, wind, west, east, levels, wind_ext, spread):
    turn_west, turn_east = info[5], info[6]
    for r in range(3):
        lanes = slice(r * WCH, (r + 1) * WCH)
        wind_ext[r, 8 : 8 + COLS] = before[:, lanes]
        wind_ext[11 + r, 8 : 8 + COLS] = after[:, lanes]
    for r in range(ROWS):
        wind_ext[3 + r, 8 : 8 + COLS] = wind[r]
    lane = lax.rem(lax.broadcasted_iota(jnp.int32, (1, WCH), 1), 2 * LEV)
    for turn, payload, first in ((turn_west, west, 4), (turn_east, east, 8 + COLS)):
        sign = jnp.where((lane >= LEV) & (turn != 0), -1.0, 1.0)
        for r in range(SIDE):
            line = payload[SIDE + r // 4, :, r % 4 * WCH : (r % 4 + 1) * WCH] * sign
            wind_ext[jnp.where(turn == 0, r, SIDE - 1 - r), first : first + 4] = line
    repeat_winds(wind_ext, levels, slice(512, 512 + PART), spread)


def frame_winds(info, *arrays):
    vmem = pl.BlockSpec(memory_space=pltpu.VMEM)
    return pl.pallas_call(
        frame_kernel,
        out_shape=[
            jax.ShapeDtypeStruct((SIDE, SPAN, WCH), jnp.float32),
            jax.ShapeDtypeStruct((2 * NSLAB, SIDE, SPAN, PART), jnp.float32),
        ],
        in_specs=[pl.BlockSpec(memory_space=pltpu.SMEM)] + [vmem] * 6,
        out_specs=[vmem] * 2,
        compiler_params=pltpu.CompilerParams(vmem_limit_bytes=24 << 20),
        cost_estimate=pl.CostEstimate(flops=16 << 30, bytes_accessed=4 << 20, transcendentals=0),
        name="frame",
    )(info, *arrays)


def window_kernel(
    part, info, wind_ids, cosine,
    before_edge, low, high, after_edge, west, east, wind_ext,
    levels, mix, basis_main, basis_rest, a_0, b_0,
    *others,
):
    a_1, b_1, earlier = others[:3] if part else (None, None, None)
    out, mine, theirs, state_a, state_b, weighted, gram, rest, *spread = others[3 * part :]
    spread = spread[0] if spread else None
    flip, mx, my, mz, mc, turn_west, turn_east = (info[i] for i in range(7))
    lanes = slice(part * 512, part * 512 + PART)
    skip = part * 64

    for r in range(4):
        state_a[4 + r, FIRST : FIRST + COLS] = low[r, :, lanes]
        state_a[8 + r, FIRST : FIRST + COLS] = high[r, :, lanes]
        for row, edge, flag in ((r, before_edge, 1 - info[7]), (12 + r, after_edge, info[7])):
            middle = slice(FIRST + 4, FIRST + COLS - 4)
            if part:
                state_a[row, middle, :128] = jnp.where(flag == 0, a_0[r, :, 512:], b_0[r, :, 512:])
                state_a[row, middle, 128:] = jnp.where(flag == 0, a_1[r], b_1[r])
            else:
                state_a[row, middle] = jnp.where(flag == 0, a_0[r], b_0[r])
            for m in range(PART // 128):
                tile = slice(m * 128, (m + 1) * 128)
                where = edge_tile(r, m + part * 4)
                ends = edge[where[0], where[1]]
                state_a[row, FIRST : FIRST + 4, tile] = ends[:4]
                state_a[row, FIRST + COLS - 4 : FIRST + COLS, tile] = ends[4:]
    for r in range(SIDE):
        from_west = jnp.where(turn_west == 0, r, SIDE - 1 - r)
        from_east = jnp.where(turn_east == 0, r, SIDE - 1 - r)
        state_a[1 + r, FIRST - 4 : FIRST] = west[from_west, :, lanes]
        state_a[1 + r, FIRST + COLS : FIRST + COLS + 4] = east[from_east, :, lanes]

    if part:
        spread = wind_ext
    else:
        repeat_winds(wind_ext, levels, lanes, spread)

    up, down = mix[0:1, lanes], mix[1:2, lanes]

    def updated(source, slab, r, c):
        now = source[r, pl.ds(c, 8), :]
        after = source[r + 1, pl.ds(c, 8), :]
        before = source[r - 1, pl.ds(c, 8), :]
        east_side = source[r, pl.ds(c + 1, 8), :]
        west_side = source[r, pl.ds(c - 1, 8), :]
        u = spread[2 * slab, r - 1, pl.ds(c - FIRST + 8, 8), :]
        v = spread[2 * slab + 1, r - 1, pl.ds(c - FIRST + 8, 8), :]
        gain_east = jnp.maximum(u, 0.0) + DIFFUSE
        gain_after = jnp.maximum(v, 0.0) + DIFFUSE
        change = gain_east * (east_side - now) + (gain_east - u) * (west_side - now)
        change += gain_after * (after - now) + (gain_after - v) * (before - now)
        above, below = pltpu.roll(now, PART - 1, 1), pltpu.roll(now, 1, 1)
        change += up * (above - now) - down * (now - below)
        return now + change

    buffers = (state_a, state_b)
    for step in range(STEPS - 1):
        source, target = buffers[step % 2], buffers[(step + 1) % 2]
        slab = wind_ids[step]

        def body(r, carry):
            for c in range(FIRST - 8, FIRST - 8 + SPAN, 8):
                target[r, c : c + 8, :] = updated(source, slab, r, c)
            return carry

        lax.fori_loop(1 + step, EXT - 1 - step, body, 0)

    source = buffers[(STEPS - 1) % 2]
    slab = wind_ids[STEPS - 1]
    own_lanes = lax.broadcasted_iota(jnp.int32, (16, 128), 1) >= skip

    def last(r, carry):
        own = jnp.where(flip == 0, r - D, ROWS - 1 - (r - D))
        share = cosine[own]
        for c in range(0, COLS, 16):
            first = updated(source, slab, r, FIRST + c)
            second = updated(source, slab, r, FIRST + c + 8)
            both = jnp.concatenate([first, second], axis=0)
            if part:
                there = slice(c, c + 16)
                out[own, there, :512] = earlier[own, there, :512]
                out[own, there, 512:640] = jnp.where(
                    own_lanes, both[:, :128], earlier[own, there, 512:]
                )
                out[own, there, 640:] = both[:, 128:]
            else:
                out[own, c : c + 16, :] = both
            weighted[own, c : c + 16, :] = (both * share).astype(jnp.bfloat16)
        return carry

    lax.fori_loop(D, D + ROWS, last, 0)

    flat_weighted = weighted[...].reshape(ROWS * COLS, PART)
    across = (((0,), (0,)), ((), ()))
    for i in range(PART // 128):
        gram[i * 128 : (i + 1) * 128, :] = lax.dot_general(
            flat_weighted[:, i * 128 : (i + 1) * 128],
            basis_main[...],
            across,
            preferred_element_type=jnp.float32,
        )
    tail = lax.dot_general(
        basis_rest[...], flat_weighted, across, preferred_element_type=jnp.float32
    )
    for g in range(8):
        rest[g, :, :LEV] = tail[:, skip + g * LEV : skip + (g + 1) * LEV]

    def place_blocks(i, carry):
        rz, rx, ry = i // 8, (i // 2) % 4, i % 2
        z, x = (mz + rz) % 4, (mx + rx) % 4
        outer, inner = (rx, rz) if part else (rz, rx)
        at = outer * 8 + inner * 2 + ry
        a = x * 2 + (my ^ ry)
        for dc, target in ((0, mine), (1, theirs)):
            g = z * 2 + (mc ^ dc)
            target[at, :LEV] = gram[
                pl.ds(pl.multiple_of(skip + g * LEV, 8), LEV),
                pl.ds(pl.multiple_of(a * 128, 128), 128),
            ]
            target[at, LEV:] = rest[g, pl.ds(pl.multiple_of(a * 16, 16), 16), :]
        return carry

    lax.fori_loop(0, 32, place_blocks, 0, unroll=8)


def window(part, scalars, arrays):
    blocks = jax.ShapeDtypeStruct((32, BLOCK, 128), jnp.float32)
    vmem = pl.BlockSpec(memory_space=pltpu.VMEM)
    return pl.pallas_call(
        functools.partial(window_kernel, part),
        out_shape=[
            jax.ShapeDtypeStruct((ROWS, COLS, CH if part else PART), jnp.float32),
            blocks,
            blocks,
        ],
        in_specs=[pl.BlockSpec(memory_space=pltpu.SMEM)] * len(scalars) + [vmem] * len(arrays),
        out_specs=[vmem] * 3,
        scratch_shapes=[
            pltpu.VMEM((EXT, PITCH, PART), jnp.float32),
            pltpu.VMEM((EXT, PITCH, PART), jnp.float32),
            pltpu.VMEM((ROWS, COLS, PART), jnp.bfloat16),
            pltpu.VMEM((PART, 1024), jnp.float32),
            pltpu.VMEM((8, 128, 128), jnp.float32),
        ]
        + [pltpu.VMEM((2 * NSLAB, SIDE, SPAN, PART), jnp.float32)] * (1 - part),
        compiler_params=pltpu.CompilerParams(vmem_limit_bytes=(24 if part else 32) << 20),
        cost_estimate=pl.CostEstimate(flops=8 << 30, bytes_accessed=16 << 20, transcendentals=0),
        name=f"window_{part}",
    )(*scalars, *arrays)


def line_sum(parts, **axis):
    (name,) = axis
    sent = [lax.ppermute(parts[k], ALL, moved(**{name: k})) for k in (1, 2, 3)]
    return (parts[0] + sent[0]) + (sent[1] + sent[2])


def shards(pool, vec_ids, winds, wind_ids, mixing, basis):
    lat_index = lax.axis_index("lat").astype(jnp.int32)
    lon_index = lax.axis_index("lon").astype(jnp.int32)
    flip = lon_index // 8
    info = jnp.stack(
        [
            flip,
            lat_index // 2,
            lat_index % 2,
            (lon_index // 2) % 4,
            lon_index % 2,
            (lon_index % 8 == 0).astype(jnp.int32),
            (lon_index % 8 == 7).astype(jnp.int32),
            (lat_index + flip) % 2,
        ]
    )
    edge_a, edge_b = lead(info, vec_ids, pool, winds)
    edge_a, edge_b = lax.ppermute(edge_a, ALL, SWAP_A), lax.ppermute(edge_b, ALL, SWAP_B)
    before_edge = jnp.where(info[7] == 0, edge_b, edge_a)
    after_edge = jnp.where(info[7] == 0, edge_a, edge_b)
    low, high, wind, a_0, a_1, b_0, b_1, basis_main, basis_rest = pack(
        info, vec_ids, pool, winds, basis
    )
    to_east, to_west, *bulk = edges(
        (before_edge, after_edge, low, high, wind), (a_0, b_0, a_1, b_1)
    )
    west = lax.ppermute(to_east, "lon", EASTWARD)
    east = lax.ppermute(to_west, "lon", WESTWARD)
    a_0, b_0 = lax.ppermute(bulk[0], ALL, SWAP_A), lax.ppermute(bulk[1], ALL, SWAP_B)
    a_1, b_1 = lax.ppermute(bulk[2], ALL, SWAP_A), lax.ppermute(bulk[3], ALL, SWAP_B)
    levels = jnp.asarray(np.arange(CH, dtype=np.int32)[None] % LEV)
    wind_ext, spread = frame_winds(info, before_edge, after_edge, wind, west, east, levels)

    level_mix = jnp.concatenate(
        [mixing.reshape(TR, LEV - 1), jnp.zeros((TR, 1), mixing.dtype)], axis=1
    )
    upper = jnp.tile(level_mix.reshape(GROUP), VEC)
    mix = jnp.stack([upper, jnp.roll(upper, 1)])
    rows = (jnp.arange(ROWS, dtype=jnp.int32) + lat_index * ROWS).astype(jnp.float32)
    cosine = jnp.cos((rows + 0.5) * (math.pi / (ROWS * 8)) - math.pi / 2)
    scalars = (info, wind_ids, cosine)
    tile = (before_edge, low, high, after_edge, west, east)
    arrays = (levels, mix, basis_main, basis_rest, a_0, b_0)
    half, mine, theirs = window(0, scalars, (*tile, wind_ext, *arrays))
    first = mine + lax.ppermute(theirs, ALL, moved(dc=1))
    sensitivity, mine, theirs = window(
        1, scalars, (*tile, spread, *arrays, a_1, b_1, half)
    )
    second = mine + lax.ppermute(theirs, ALL, moved(dc=1))

    first = line_sum(first.reshape(4, 8, BLOCK, 128), dz=1)
    second = line_sum(second.reshape(4, 8, BLOCK, 128), dx=1)
    first = line_sum(first.reshape(4, 2, BLOCK, 128), dx=1)
    second = line_sum(second.reshape(4, 2, BLOCK, 128), dz=1)
    near = jnp.where(flip == 0, first, second)
    far = jnp.where(flip == 0, second, first)
    block = near[0] + lax.ppermute(near[1], ALL, turned(1))
    block += lax.ppermute(far[0], ALL, turned(2)) + lax.ppermute(far[1], ALL, turned(3))
    ritz = jnp.concatenate([block[:LEV].T, block[LEV:, :LEV]], axis=0)
    return sensitivity, ritz * (1.0 / math.sqrt(ROWS * COLS * 128))


def solution(mesh):
    in_specs = (P("lat", "lon", None), P(), P("lat", "lon", None), P(), P(), P("lat", "lon", None))
    out_specs = (P("lat", "lon", None), P("lat", "lon"))
    return jax.shard_map(shards, mesh=mesh, in_specs=in_specs, out_specs=out_specs, check_vma=False)
```

```python
import functools
import functools
import math

import jax
import jax.numpy as jnp
import numpy as np
from jax import lax
from jax.experimental import pallas as pl
from jax.experimental.pallas import tpu as pltpu
from jax.sharding import PartitionSpec as P

LEV = 72
TR = 2
VEC = 8
POOL = 8
NSLAB = 2
STEPS = 4
DIFFUSE = 0.075
ALL = ("lat", "lon")

ROWS = 8
COLS = 48
CH = VEC * TR * LEV
GROUP = TR * LEV
WCH = NSLAB * 2 * LEV
D = STEPS
EXT = ROWS + 2 * D
PITCH = 80
FIRST = 16
SPAN = 64
WPACK = 896
PART = 640
BLOCK = 88


def place(x, y, z, core):
    return (x * 2 + y % 2) * 16 + (y // 2) * 8 + z * 2 + core


PLACES = [(x, y, z, c) for x in range(4) for y in range(4) for z in range(4) for c in range(2)]


def moved(dx=0, dy=0, dz=0, dc=0):
    return [
        (place(x, y, z, c), place((x + dx) % 4, (y + dy) % 4, (z + dz) % 4, c ^ dc))
        for x, y, z, c in PLACES
    ]


def turned(bits):
    return [(place(x, y, z, c), place(x, y ^ bits, z, c)) for x, y, z, c in PLACES]


def meridian():
    pairs = []
    for b in range(8):
        for a in range(8):
            pairs.append((a * 16 + b, (a + 1) * 16 + b if a < 7 else a * 16 + b + 8))
            pairs.append((a * 16 + b + 8, (a - 1) * 16 + b + 8 if a > 0 else a * 16 + b))
    return pairs


FORWARD = meridian()
BACKWARD = [(t, s) for s, t in FORWARD]
CIRCLE = FORWARD + BACKWARD
SWAP_A = [(s, t) for s, t in CIRCLE if s // 16 // 2 == t // 16 // 2 and s // 16 != t // 16]
SWAP_B = [pair for pair in CIRCLE if pair not in SWAP_A]
EASTWARD = [(b, (b + 1) % 16) for b in range(16)]
WESTWARD = [(t, s) for s, t in EASTWARD]


def edge_tile(r, m):
    i = r * (CH // 128) + m
    return slice(i // 6 * 8, i // 6 * 8 + 8), slice(WPACK + i % 6 * 128, WPACK + i % 6 * 128 + 128)


def choose(vec_ids, chosen):
    lane = lax.broadcasted_iota(jnp.int32, (1, CH), 1)
    source = lane
    for k in range(VEC):
        inside = (lane >= k * GROUP) & (lane < (k + 1) * GROUP)
        source = jnp.where(inside, lane + (vec_ids[k] - k) * GROUP, source)
    for i in range(CH // 128):
        row = lax.broadcasted_iota(jnp.int32, (128, CH), 0) + i * 128
        chosen[i * 128 : (i + 1) * 128, :] = jnp.where(row == source, 1.0, 0.0).astype(jnp.bfloat16)


def turned_wind(winds, info, r):
    place_in_slab = lax.rem(lax.broadcasted_iota(jnp.int32, (1, WCH), 1), 2 * LEV)
    turn = jnp.where((place_in_slab >= LEV) & (info[0] != 0), -1.0, 1.0)
    return winds[jnp.where(info[0] == 0, r, ROWS - 1 - r)] * turn


def lead_kernel(
    info, vec_ids, pool, winds, edge_next, edge_last, chosen, ends, held_winds, made, sems
):
    fetch = [
        pltpu.make_async_copy(pool.at[:, :16, :], ends.at[0], sems.at[0]),
        pltpu.make_async_copy(pool.at[:, COLS - 16 :, :], ends.at[1], sems.at[1]),
        pltpu.make_async_copy(winds, held_winds, sems.at[2]),
    ]
    for copy in fetch:
        copy.start()
    choose(vec_ids, chosen)
    for copy in fetch:
        copy.wait()
    for i in range(2):
        rows = ends[i].reshape(ROWS * 16, CH)
        picked = jnp.dot(rows, chosen[...], preferred_element_type=jnp.float32)
        made[i] = picked.reshape(ROWS, 16, CH)
    for r in range(4):
        for edge, end in ((edge_next, 1), (edge_last, 0)):
            row = end * 4 + r
            own = jnp.where(info[0] == 0, row, ROWS - 1 - row)
            for m in range(CH // 128):
                lanes = slice(m * 128, (m + 1) * 128)
                where = edge_tile(r, m)
                edge[where[0], where[1]] = jnp.concatenate(
                    [made[0, own, :4, lanes], made[1, own, 12:, lanes]], axis=0
                )
    for r in range(3):
        lanes = slice(r * WCH, (r + 1) * WCH)
        for edge, end in ((edge_next, 1), (edge_last, 0)):
            row = end * (ROWS - 3) + r
            edge[:, lanes] = turned_wind(held_winds, info, row)


def lead(info, vec_ids, pool, winds):
    vmem = pl.BlockSpec(memory_space=pltpu.VMEM)
    return pl.pallas_call(
        lead_kernel,
        out_shape=[jax.ShapeDtypeStruct((COLS, WPACK + 768), jnp.float32)] * 2,
        in_specs=[pl.BlockSpec(memory_space=pltpu.SMEM)] * 2
        + [pl.BlockSpec(memory_space=pltpu.HBM)] * 2,
        out_specs=[vmem] * 2,
        scratch_shapes=[
            pltpu.VMEM((CH, CH), jnp.bfloat16),
            pltpu.VMEM((2, ROWS, 16, CH), jnp.bfloat16),
            pltpu.VMEM((ROWS, COLS, WCH), jnp.float32),
            pltpu.VMEM((2, ROWS, 16, CH), jnp.float32),
            pltpu.SemaphoreType.DMA((3,)),
        ],
        compiler_params=pltpu.CompilerParams(vmem_limit_bytes=60 << 20),
        cost_estimate=pl.CostEstimate(flops=1 << 30, bytes_accessed=4 << 20, transcendentals=0),
        name="lead",
    )(info, vec_ids, pool, winds)


def pack_kernel(
    info, vec_ids, pool, winds, basis,
    low, high, wind, a_0, a_1, b_0, b_1, basis_main, basis_rest, chosen,
):
    choose(vec_ids, chosen)
    for half in range(2):
        rows = pool[half * 4 : half * 4 + 4].reshape(4 * COLS, CH)
        picked = jnp.dot(rows, chosen[...], preferred_element_type=jnp.float32)
        picked = picked.reshape(4, COLS, CH)

        @pl.when(info[0] == 0)
        def _():
            (low, high)[half][...] = picked

        @pl.when(info[0] != 0)
        def _():
            for r in range(4):
                (high, low)[half][3 - r] = picked[r]

    for flag, bulk_0, bulk_1 in ((info[7], a_0, a_1), (1 - info[7], b_0, b_1)):
        for r in range(4):
            line = jnp.where(flag == 0, high[r, 4 : COLS - 4, :], low[r, 4 : COLS - 4, :])
            bulk_0[r] = line[:, :PART]
            bulk_1[r] = line[:, PART:]
    for r in range(ROWS):
        wind[r] = turned_wind(winds, info, r)
    flat = basis[...].reshape(ROWS * COLS, CH)
    for a in range(8):
        basis_main[:, a * 128 : (a + 1) * 128] = flat[:, a * 144 : a * 144 + 128]
        basis_rest[:, a * 16 : (a + 1) * 16] = flat[:, a * 144 + 128 : (a + 1) * 144]


def pack(info, vec_ids, pool, winds, basis):
    shapes = [(4, COLS, CH)] * 2 + [(ROWS, COLS, WCH)]
    shapes += [(4, COLS - 8, PART), (4, COLS - 8, CH - PART)] * 2
    outs = [jax.ShapeDtypeStruct(s, jnp.float32) for s in shapes]
    outs += [jax.ShapeDtypeStruct((ROWS * COLS, n), jnp.bfloat16) for n in (1024, 128)]
    vmem = pl.BlockSpec(memory_space=pltpu.VMEM)
    return pl.pallas_call(
        pack_kernel,
        out_shape=outs,
        in_specs=[pl.BlockSpec(memory_space=pltpu.SMEM)] * 2 + [vmem] * 3,
        out_specs=[vmem] * 9,
        scratch_shapes=[pltpu.VMEM((CH, CH), jnp.bfloat16)],
        compiler_params=pltpu.CompilerParams(vmem_limit_bytes=24 << 20),
        cost_estimate=pl.CostEstimate(flops=1 << 30, bytes_accessed=4 << 20, transcendentals=0),
        name="pack",
    )(info, vec_ids, pool, winds, basis)


SIDE = EXT - 2


def edges_kernel(before, after, low, high, wind, *rest):
    to_east, to_west = rest[4:6]
    for first, near, target in ((COLS - 4, 4, to_east), (0, 0, to_west)):
        columns = slice(first, first + 4)
        for r in range(3):
            for m in range(CH // 128):
                lanes = slice(m * 128, (m + 1) * 128)
                where = edge_tile(r + 1, m)
                target[r, :, lanes] = before[where[0], where[1]][near : near + 4]
                where = edge_tile(r, m)
                target[11 + r, :, lanes] = after[where[0], where[1]][near : near + 4]
        for r in range(4):
            target[3 + r] = low[r, columns, :]
            target[7 + r] = high[r, columns, :]
        for r in range(SIDE):
            if r < 3:
                line = before[columns, r * WCH : (r + 1) * WCH]
            elif r < 11:
                line = wind[r - 3, columns, :]
            else:
                line = after[columns, (r - 11) * WCH : (r - 10) * WCH]
            target[SIDE + r // 4, :, r % 4 * WCH : (r % 4 + 1) * WCH] = line


def edges(arrays, bulk):
    vmem = pl.BlockSpec(memory_space=pltpu.VMEM)
    anywhere = pl.BlockSpec(memory_space=pl.ANY)
    shapes = [jax.ShapeDtypeStruct((SIDE + 4, 4, CH), jnp.float32)] * 2
    return pl.pallas_call(
        edges_kernel,
        out_shape=shapes + [jax.ShapeDtypeStruct(b.shape, b.dtype) for b in bulk],
        in_specs=[vmem] * 5 + [anywhere] * 4,
        out_specs=[vmem] * 2 + [anywhere] * 4,
        input_output_aliases={5 + i: 2 + i for i in range(4)},
        compiler_params=pltpu.CompilerParams(vmem_limit_bytes=16 << 20),
        cost_estimate=pl.CostEstimate(flops=1 << 20, bytes_accessed=4 << 20, transcendentals=0),
        name="edges",
    )(*arrays, *bulk)


def repeat_winds(wind_ext, levels, lanes, spread):
    level = lax.broadcasted_iota(jnp.int32, (2 * LEV, PART), 0)
    level = jnp.where(level >= LEV, level - LEV, level)
    repeat = jnp.where(level == levels[:, lanes], 1.0, 0.0).astype(jnp.bfloat16)
    flat = wind_ext[...].reshape(SIDE * SPAN, WCH)
    for i in range(2 * NSLAB):
        value = flat[:, i * LEV : (i + 1) * LEV]
        coarse = value.astype(jnp.bfloat16)
        fine = (value - coarse.astype(jnp.float32)).astype(jnp.bfloat16)
        both = jnp.concatenate([coarse, fine], axis=1)
        spread[i] = jnp.dot(both, repeat, preferred_element_type=jnp.float32).reshape(
            SIDE, SPAN, PART
        )


def frame_kernel(info, before, after, wind, west, east, levels, wind_ext, spread):
    turn_west, turn_east = info[5], info[6]
    for r in range(3):
        lanes = slice(r * WCH, (r + 1) * WCH)
        wind_ext[r, 8 : 8 + COLS] = before[:, lanes]
        wind_ext[11 + r, 8 : 8 + COLS] = after[:, lanes]
    for r in range(ROWS):
        wind_ext[3 + r, 8 : 8 + COLS] = wind[r]
    lane = lax.rem(lax.broadcasted_iota(jnp.int32, (1, WCH), 1), 2 * LEV)
    for turn, payload, first in ((turn_west, west, 4), (turn_east, east, 8 + COLS)):
        sign = jnp.where((lane >= LEV) & (turn != 0), -1.0, 1.0)
        for r in range(SIDE):
            line = payload[SIDE + r // 4, :, r % 4 * WCH : (r % 4 + 1) * WCH] * sign
            wind_ext[jnp.where(turn == 0, r, SIDE - 1 - r), first : first + 4] = line
    repeat_winds(wind_ext, levels, slice(512, 512 + PART), spread)


def frame_winds(info, *arrays):
    vmem = pl.BlockSpec(memory_space=pltpu.VMEM)
    return pl.pallas_call(
        frame_kernel,
        out_shape=[
            jax.ShapeDtypeStruct((SIDE, SPAN, WCH), jnp.float32),
            jax.ShapeDtypeStruct((2 * NSLAB, SIDE, SPAN, PART), jnp.float32),
        ],
        in_specs=[pl.BlockSpec(memory_space=pltpu.SMEM)] + [vmem] * 6,
        out_specs=[vmem] * 2,
        compiler_params=pltpu.CompilerParams(vmem_limit_bytes=24 << 20),
        cost_estimate=pl.CostEstimate(flops=16 << 30, bytes_accessed=4 << 20, transcendentals=0),
        name="frame",
    )(info, *arrays)


def window_kernel(
    part, info, wind_ids, cosine,
    before_edge, low, high, after_edge, west, east, wind_ext,
    levels, mix, basis_main, basis_rest, a_0, b_0,
    *others,
):
    a_1, b_1, earlier = others[:3] if part else (None, None, None)
    out, mine, theirs, state_a, state_b, weighted, gram, rest, *spread = others[3 * part :]
    spread = spread[0] if spread else None
    flip, mx, my, mz, mc, turn_west, turn_east = (info[i] for i in range(7))
    lanes = slice(part * 512, part * 512 + PART)
    skip = part * 64

    for r in range(4):
        state_a[4 + r, FIRST : FIRST + COLS] = low[r, :, lanes]
        state_a[8 + r, FIRST : FIRST + COLS] = high[r, :, lanes]
        for row, edge, flag in ((r, before_edge, 1 - info[7]), (12 + r, after_edge, info[7])):
            middle = slice(FIRST + 4, FIRST + COLS - 4)
            if part:
                state_a[row, middle, :128] = jnp.where(flag == 0, a_0[r, :, 512:], b_0[r, :, 512:])
                state_a[row, middle, 128:] = jnp.where(flag == 0, a_1[r], b_1[r])
            else:
                state_a[row, middle] = jnp.where(flag == 0, a_0[r], b_0[r])
            for m in range(PART // 128):
                tile = slice(m * 128, (m + 1) * 128)
                where = edge_tile(r, m + part * 4)
                ends = edge[where[0], where[1]]
                state_a[row, FIRST : FIRST + 4, tile] = ends[:4]
                state_a[row, FIRST + COLS - 4 : FIRST + COLS, tile] = ends[4:]
    for r in range(SIDE):
        from_west = jnp.where(turn_west == 0, r, SIDE - 1 - r)
        from_east = jnp.where(turn_east == 0, r, SIDE - 1 - r)
        state_a[1 + r, FIRST - 4 : FIRST] = west[from_west, :, lanes]
        state_a[1 + r, FIRST + COLS : FIRST + COLS + 4] = east[from_east, :, lanes]

    if part:
        spread = wind_ext
    else:
        repeat_winds(wind_ext, levels, lanes, spread)

    up, down = mix[0:1, lanes], mix[1:2, lanes]

    def updated(source, slab, r, c):
        now = source[r, pl.ds(c, 8), :]
        after = source[r + 1, pl.ds(c, 8), :]
        before = source[r - 1, pl.ds(c, 8), :]
        east_side = source[r, pl.ds(c + 1, 8), :]
        west_side = source[r, pl.ds(c - 1, 8), :]
        u = spread[2 * slab, r - 1, pl.ds(c - FIRST + 8, 8), :]
        v = spread[2 * slab + 1, r - 1, pl.ds(c - FIRST + 8, 8), :]
        gain_east = jnp.maximum(u, 0.0) + DIFFUSE
        gain_after = jnp.maximum(v, 0.0) + DIFFUSE
        change = gain_east * (east_side - now) + (gain_east - u) * (west_side - now)
        change += gain_after * (after - now) + (gain_after - v) * (before - now)
        above, below = pltpu.roll(now, PART - 1, 1), pltpu.roll(now, 1, 1)
        change += up * (above - now) - down * (now - below)
        return now + change

    buffers = (state_a, state_b)
    for step in range(STEPS - 1):
        source, target = buffers[step % 2], buffers[(step + 1) % 2]
        slab = wind_ids[step]

        def body(r, carry):
            for c in range(FIRST - 8, FIRST - 8 + SPAN, 8):
                target[r, c : c + 8, :] = updated(source, slab, r, c)
            return carry

        lax.fori_loop(1 + step, EXT - 1 - step, body, 0)

    source = buffers[(STEPS - 1) % 2]
    slab = wind_ids[STEPS - 1]
    own_lanes = lax.broadcasted_iota(jnp.int32, (16, 128), 1) >= skip

    def last(r, carry):
        own = jnp.where(flip == 0, r - D, ROWS - 1 - (r - D))
        share = cosine[own]
        for c in range(0, COLS, 16):
            first = updated(source, slab, r, FIRST + c)
            second = updated(source, slab, r, FIRST + c + 8)
            both = jnp.concatenate([first, second], axis=0)
            if part:
                there = slice(c, c + 16)
                out[own, there, :512] = earlier[own, there, :512]
                out[own, there, 512:640] = jnp.where(
                    own_lanes, both[:, :128], earlier[own, there, 512:]
                )
                out[own, there, 640:] = both[:, 128:]
            else:
                out[own, c : c + 16, :] = both
            weighted[own, c : c + 16, :] = (both * share).astype(jnp.bfloat16)
        return carry

    lax.fori_loop(D, D + ROWS, last, 0)

    flat_weighted = weighted[...].reshape(ROWS * COLS, PART)
    across = (((0,), (0,)), ((), ()))
    for i in range(PART // 128):
        gram[i * 128 : (i + 1) * 128, :] = lax.dot_general(
            flat_weighted[:, i * 128 : (i + 1) * 128],
            basis_main[...],
            across,
            preferred_element_type=jnp.float32,
        )
    tail = lax.dot_general(
        basis_rest[...], flat_weighted, across, preferred_element_type=jnp.float32
    )
    for g in range(8):
        rest[g, :, :LEV] = tail[:, skip + g * LEV : skip + (g + 1) * LEV]

    def place_blocks(i, carry):
        rz, rx, ry = i // 8, (i // 2) % 4, i % 2
        z, x = (mz + rz) % 4, (mx + rx) % 4
        outer, inner = (rx, rz) if part else (rz, rx)
        at = outer * 8 + inner * 2 + ry
        a = x * 2 + (my ^ ry)
        for dc, target in ((0, mine), (1, theirs)):
            g = z * 2 + (mc ^ dc)
            target[at, :LEV] = gram[
                pl.ds(pl.multiple_of(skip + g * LEV, 8), LEV),
                pl.ds(pl.multiple_of(a * 128, 128), 128),
            ]
            target[at, LEV:] = rest[g, pl.ds(pl.multiple_of(a * 16, 16), 16), :]
        return carry

    lax.fori_loop(0, 32, place_blocks, 0, unroll=8)


def window(part, scalars, arrays):
    blocks = jax.ShapeDtypeStruct((32, BLOCK, 128), jnp.float32)
    vmem = pl.BlockSpec(memory_space=pltpu.VMEM)
    return pl.pallas_call(
        functools.partial(window_kernel, part),
        out_shape=[
            jax.ShapeDtypeStruct((ROWS, COLS, CH if part else PART), jnp.float32),
            blocks,
            blocks,
        ],
        in_specs=[pl.BlockSpec(memory_space=pltpu.SMEM)] * len(scalars) + [vmem] * len(arrays),
        out_specs=[vmem] * 3,
        scratch_shapes=[
            pltpu.VMEM((EXT, PITCH, PART), jnp.float32),
            pltpu.VMEM((EXT, PITCH, PART), jnp.float32),
            pltpu.VMEM((ROWS, COLS, PART), jnp.bfloat16),
            pltpu.VMEM((PART, 1024), jnp.float32),
            pltpu.VMEM((8, 128, 128), jnp.float32),
        ]
        + [pltpu.VMEM((2 * NSLAB, SIDE, SPAN, PART), jnp.float32)] * (1 - part),
        compiler_params=pltpu.CompilerParams(vmem_limit_bytes=(24 if part else 32) << 20),
        cost_estimate=pl.CostEstimate(flops=8 << 30, bytes_accessed=16 << 20, transcendentals=0),
        name=f"window_{part}",
    )(*scalars, *arrays)


def line_sum(parts, **axis):
    (name,) = axis
    sent = [lax.ppermute(parts[k], ALL, moved(**{name: k})) for k in (1, 2, 3)]
    return (parts[0] + sent[0]) + (sent[1] + sent[2])


def shards(pool, vec_ids, winds, wind_ids, mixing, basis):
    lat_index = lax.axis_index("lat").astype(jnp.int32)
    lon_index = lax.axis_index("lon").astype(jnp.int32)
    flip = lon_index // 8
    info = jnp.stack(
        [
            flip,
            lat_index // 2,
            lat_index % 2,
            (lon_index // 2) % 4,
            lon_index % 2,
            (lon_index % 8 == 0).astype(jnp.int32),
            (lon_index % 8 == 7).astype(jnp.int32),
            (lat_index + flip) % 2,
        ]
    )
    edge_next, edge_last = lead(info, vec_ids, pool, winds)
    before_edge = lax.ppermute(edge_next, ALL, FORWARD)
    after_edge = lax.ppermute(edge_last, ALL, BACKWARD)
    low, high, wind, a_0, a_1, b_0, b_1, basis_main, basis_rest = pack(
        info, vec_ids, pool, winds, basis
    )
    to_east, to_west, *bulk = edges(
        (before_edge, after_edge, low, high, wind), (a_0, b_0, a_1, b_1)
    )
    west = lax.ppermute(to_east, "lon", EASTWARD)
    east = lax.ppermute(to_west, "lon", WESTWARD)
    a_0, b_0 = lax.ppermute(bulk[0], ALL, SWAP_A), lax.ppermute(bulk[1], ALL, SWAP_B)
    a_1, b_1 = lax.ppermute(bulk[2], ALL, SWAP_A), lax.ppermute(bulk[3], ALL, SWAP_B)
    levels = jnp.asarray(np.arange(CH, dtype=np.int32)[None] % LEV)
    wind_ext, spread = frame_winds(info, before_edge, after_edge, wind, west, east, levels)

    level_mix = jnp.concatenate(
        [mixing.reshape(TR, LEV - 1), jnp.zeros((TR, 1), mixing.dtype)], axis=1
    )
    upper = jnp.tile(level_mix.reshape(GROUP), VEC)
    mix = jnp.stack([upper, jnp.roll(upper, 1)])
    rows = (jnp.arange(ROWS, dtype=jnp.int32) + lat_index * ROWS).astype(jnp.float32)
    cosine = jnp.cos((rows + 0.5) * (math.pi / (ROWS * 8)) - math.pi / 2)
    scalars = (info, wind_ids, cosine)
    tile = (before_edge, low, high, after_edge, west, east)
    arrays = (levels, mix, basis_main, basis_rest, a_0, b_0)
    half, mine, theirs = window(0, scalars, (*tile, wind_ext, *arrays))
    first = mine + lax.ppermute(theirs, ALL, moved(dc=1))
    sensitivity, mine, theirs = window(
        1, scalars, (*tile, spread, *arrays, a_1, b_1, half)
    )
    second = mine + lax.ppermute(theirs, ALL, moved(dc=1))

    first = line_sum(first.reshape(4, 8, BLOCK, 128), dz=1)
    second = line_sum(second.reshape(4, 8, BLOCK, 128), dx=1)
    first = line_sum(first.reshape(4, 2, BLOCK, 128), dx=1)
    second = line_sum(second.reshape(4, 2, BLOCK, 128), dz=1)
    near = jnp.where(flip == 0, first, second)
    far = jnp.where(flip == 0, second, first)
    block = near[0] + lax.ppermute(near[1], ALL, turned(1))
    block += lax.ppermute(far[0], ALL, turned(2)) + lax.ppermute(far[1], ALL, turned(3))
    ritz = jnp.concatenate([block[:LEV].T, block[LEV:, :LEV]], axis=0)
    return sensitivity, ritz * (1.0 / math.sqrt(ROWS * COLS * 128))


def solution(mesh):
    in_specs = (P("lat", "lon", None), P(), P("lat", "lon", None), P(), P(), P("lat", "lon", None))
    out_specs = (P("lat", "lon", None), P("lat", "lon"))
    return jax.shard_map(shards, mesh=mesh, in_specs=in_specs, out_specs=out_specs, check_vma=False)
```

```python
import functools
import functools
import math

import jax
import jax.numpy as jnp
import numpy as np
from jax import lax
from jax.experimental import pallas as pl
from jax.experimental.pallas import tpu as pltpu
from jax.sharding import PartitionSpec as P

LEV = 72
TR = 2
VEC = 8
POOL = 8
NSLAB = 2
STEPS = 4
DIFFUSE = 0.075
ALL = ("lat", "lon")

ROWS = 8
COLS = 48
CH = VEC * TR * LEV
GROUP = TR * LEV
WCH = NSLAB * 2 * LEV
D = STEPS
EXT = ROWS + 2 * D
PITCH = 80
FIRST = 16
SPAN = 64
WPACK = 896
PART = 640
BLOCK = 88


def place(x, y, z, core):
    return (x * 2 + y % 2) * 16 + (y // 2) * 8 + z * 2 + core


PLACES = [(x, y, z, c) for x in range(4) for y in range(4) for z in range(4) for c in range(2)]


def moved(dx=0, dy=0, dz=0, dc=0):
    return [
        (place(x, y, z, c), place((x + dx) % 4, (y + dy) % 4, (z + dz) % 4, c ^ dc))
        for x, y, z, c in PLACES
    ]


def turned(bits):
    return [(place(x, y, z, c), place(x, y ^ bits, z, c)) for x, y, z, c in PLACES]


def meridian():
    pairs = []
    for b in range(8):
        for a in range(8):
            pairs.append((a * 16 + b, (a + 1) * 16 + b if a < 7 else a * 16 + b + 8))
            pairs.append((a * 16 + b + 8, (a - 1) * 16 + b + 8 if a > 0 else a * 16 + b))
    return pairs


FORWARD = meridian()
BACKWARD = [(t, s) for s, t in FORWARD]
EASTWARD = [(b, (b + 1) % 16) for b in range(16)]
WESTWARD = [(t, s) for s, t in EASTWARD]


def edge_tile(r, m):
    i = r * (CH // 128) + m
    return slice(i // 6 * 8, i // 6 * 8 + 8), slice(WPACK + i % 6 * 128, WPACK + i % 6 * 128 + 128)


def choose(vec_ids, chosen):
    lane = lax.broadcasted_iota(jnp.int32, (1, CH), 1)
    source = lane
    for k in range(VEC):
        inside = (lane >= k * GROUP) & (lane < (k + 1) * GROUP)
        source = jnp.where(inside, lane + (vec_ids[k] - k) * GROUP, source)
    for i in range(CH // 128):
        row = lax.broadcasted_iota(jnp.int32, (128, CH), 0) + i * 128
        chosen[i * 128 : (i + 1) * 128, :] = jnp.where(row == source, 1.0, 0.0).astype(jnp.bfloat16)


def turned_wind(winds, info, r):
    place_in_slab = lax.rem(lax.broadcasted_iota(jnp.int32, (1, WCH), 1), 2 * LEV)
    turn = jnp.where((place_in_slab >= LEV) & (info[0] != 0), -1.0, 1.0)
    return winds[jnp.where(info[0] == 0, r, ROWS - 1 - r)] * turn


def lead_kernel(
    info, vec_ids, pool, winds, edge_next, edge_last, chosen, ends, held_winds, made, sems
):
    fetch = [
        pltpu.make_async_copy(pool.at[:, :16, :], ends.at[0], sems.at[0]),
        pltpu.make_async_copy(pool.at[:, COLS - 16 :, :], ends.at[1], sems.at[1]),
        pltpu.make_async_copy(winds, held_winds, sems.at[2]),
    ]
    for copy in fetch:
        copy.start()
    choose(vec_ids, chosen)
    for copy in fetch:
        copy.wait()
    for i in range(2):
        rows = ends[i].reshape(ROWS * 16, CH)
        picked = jnp.dot(rows, chosen[...], preferred_element_type=jnp.float32)
        made[i] = picked.reshape(ROWS, 16, CH)
    for r in range(4):
        for edge, row in ((edge_last, r), (edge_next, 4 + r)):
            own = jnp.where(info[0] == 0, row, ROWS - 1 - row)
            for m in range(CH // 128):
                lanes = slice(m * 128, (m + 1) * 128)
                where = edge_tile(r, m)
                edge[where[0], where[1]] = jnp.concatenate(
                    [made[0, own, :4, lanes], made[1, own, 12:, lanes]], axis=0
                )
    for r in range(3):
        lanes = slice(r * WCH, (r + 1) * WCH)
        edge_last[:, lanes] = turned_wind(held_winds, info, r)
        edge_next[:, lanes] = turned_wind(held_winds, info, ROWS - 3 + r)


def lead(info, vec_ids, pool, winds):
    vmem = pl.BlockSpec(memory_space=pltpu.VMEM)
    return pl.pallas_call(
        lead_kernel,
        out_shape=[jax.ShapeDtypeStruct((COLS, WPACK + 768), jnp.float32)] * 2,
        in_specs=[pl.BlockSpec(memory_space=pltpu.SMEM)] * 2
        + [pl.BlockSpec(memory_space=pltpu.HBM)] * 2,
        out_specs=[vmem] * 2,
        scratch_shapes=[
            pltpu.VMEM((CH, CH), jnp.bfloat16),
            pltpu.VMEM((2, ROWS, 16, CH), jnp.bfloat16),
            pltpu.VMEM((ROWS, COLS, WCH), jnp.float32),
            pltpu.VMEM((2, ROWS, 16, CH), jnp.float32),
            pltpu.SemaphoreType.DMA((3,)),
        ],
        compiler_params=pltpu.CompilerParams(vmem_limit_bytes=60 << 20),
        cost_estimate=pl.CostEstimate(flops=1 << 30, bytes_accessed=4 << 20, transcendentals=0),
        name="lead",
    )(info, vec_ids, pool, winds)


def pack_kernel(
    info, vec_ids, pool, winds, basis,
    low, high, wind, next_0, next_1, last_0, last_1, basis_main, basis_rest, chosen,
):
    choose(vec_ids, chosen)
    for half in range(2):
        rows = pool[half * 4 : half * 4 + 4].reshape(4 * COLS, CH)
        picked = jnp.dot(rows, chosen[...], preferred_element_type=jnp.float32)
        picked = picked.reshape(4, COLS, CH)

        @pl.when(info[0] == 0)
        def _():
            (low, high)[half][...] = picked

        @pl.when(info[0] != 0)
        def _():
            for r in range(4):
                (high, low)[half][3 - r] = picked[r]

    for rows, bulk_0, bulk_1 in ((high, next_0, next_1), (low, last_0, last_1)):
        for r in range(4):
            bulk_0[r] = rows[r, 4 : COLS - 4, :PART]
            bulk_1[r] = rows[r, 4 : COLS - 4, PART:]
    for r in range(ROWS):
        wind[r] = turned_wind(winds, info, r)
    flat = basis[...].reshape(ROWS * COLS, CH)
    for a in range(8):
        basis_main[:, a * 128 : (a + 1) * 128] = flat[:, a * 144 : a * 144 + 128]
        basis_rest[:, a * 16 : (a + 1) * 16] = flat[:, a * 144 + 128 : (a + 1) * 144]


def pack(info, vec_ids, pool, winds, basis):
    shapes = [(4, COLS, CH)] * 2 + [(ROWS, COLS, WCH)]
    shapes += [(4, COLS - 8, PART), (4, COLS - 8, CH - PART)] * 2
    outs = [jax.ShapeDtypeStruct(s, jnp.float32) for s in shapes]
    outs += [jax.ShapeDtypeStruct((ROWS * COLS, n), jnp.bfloat16) for n in (1024, 128)]
    vmem = pl.BlockSpec(memory_space=pltpu.VMEM)
    return pl.pallas_call(
        pack_kernel,
        out_shape=outs,
        in_specs=[pl.BlockSpec(memory_space=pltpu.SMEM)] * 2 + [vmem] * 3,
        out_specs=[vmem] * 9,
        scratch_shapes=[pltpu.VMEM((CH, CH), jnp.bfloat16)],
        compiler_params=pltpu.CompilerParams(vmem_limit_bytes=24 << 20),
        cost_estimate=pl.CostEstimate(flops=1 << 30, bytes_accessed=4 << 20, transcendentals=0),
        name="pack",
    )(info, vec_ids, pool, winds, basis)


SIDE = EXT - 2


def edges_kernel(before, after, low, high, wind, *rest):
    to_east, to_west = rest[4:6]
    for first, near, target in ((COLS - 4, 4, to_east), (0, 0, to_west)):
        columns = slice(first, first + 4)
        for r in range(3):
            for m in range(CH // 128):
                lanes = slice(m * 128, (m + 1) * 128)
                where = edge_tile(r + 1, m)
                target[r, :, lanes] = before[where[0], where[1]][near : near + 4]
                where = edge_tile(r, m)
                target[11 + r, :, lanes] = after[where[0], where[1]][near : near + 4]
        for r in range(4):
            target[3 + r] = low[r, columns, :]
            target[7 + r] = high[r, columns, :]
        for r in range(SIDE):
            if r < 3:
                line = before[columns, r * WCH : (r + 1) * WCH]
            elif r < 11:
                line = wind[r - 3, columns, :]
            else:
                line = after[columns, (r - 11) * WCH : (r - 10) * WCH]
            target[SIDE + r // 4, :, r % 4 * WCH : (r % 4 + 1) * WCH] = line


def edges(arrays, bulk):
    vmem = pl.BlockSpec(memory_space=pltpu.VMEM)
    anywhere = pl.BlockSpec(memory_space=pl.ANY)
    shapes = [jax.ShapeDtypeStruct((SIDE + 4, 4, CH), jnp.float32)] * 2
    return pl.pallas_call(
        edges_kernel,
        out_shape=shapes + [jax.ShapeDtypeStruct(b.shape, b.dtype) for b in bulk],
        in_specs=[vmem] * 5 + [anywhere] * 4,
        out_specs=[vmem] * 2 + [anywhere] * 4,
        input_output_aliases={5 + i: 2 + i for i in range(4)},
        compiler_params=pltpu.CompilerParams(vmem_limit_bytes=16 << 20),
        cost_estimate=pl.CostEstimate(flops=1 << 20, bytes_accessed=4 << 20, transcendentals=0),
        name="edges",
    )(*arrays, *bulk)


def repeat_winds(wind_ext, levels, lanes, spread):
    level = lax.broadcasted_iota(jnp.int32, (2 * LEV, PART), 0)
    level = jnp.where(level >= LEV, level - LEV, level)
    repeat = jnp.where(level == levels[:, lanes], 1.0, 0.0).astype(jnp.bfloat16)
    flat = wind_ext[...].reshape(SIDE * SPAN, WCH)
    for i in range(2 * NSLAB):
        value = flat[:, i * LEV : (i + 1) * LEV]
        coarse = value.astype(jnp.bfloat16)
        fine = (value - coarse.astype(jnp.float32)).astype(jnp.bfloat16)
        both = jnp.concatenate([coarse, fine], axis=1)
        spread[i] = jnp.dot(both, repeat, preferred_element_type=jnp.float32).reshape(
            SIDE, SPAN, PART
        )


def frame_kernel(info, before, after, wind, west, east, levels, wind_ext, spread):
    turn_west, turn_east = info[5], info[6]
    for r in range(3):
        lanes = slice(r * WCH, (r + 1) * WCH)
        wind_ext[r, 8 : 8 + COLS] = before[:, lanes]
        wind_ext[11 + r, 8 : 8 + COLS] = after[:, lanes]
    for r in range(ROWS):
        wind_ext[3 + r, 8 : 8 + COLS] = wind[r]
    lane = lax.rem(lax.broadcasted_iota(jnp.int32, (1, WCH), 1), 2 * LEV)
    for turn, payload, first in ((turn_west, west, 4), (turn_east, east, 8 + COLS)):
        sign = jnp.where((lane >= LEV) & (turn != 0), -1.0, 1.0)
        for r in range(SIDE):
            line = payload[SIDE + r // 4, :, r % 4 * WCH : (r % 4 + 1) * WCH] * sign
            wind_ext[jnp.where(turn == 0, r, SIDE - 1 - r), first : first + 4] = line
    repeat_winds(wind_ext, levels, slice(512, 512 + PART), spread)


def frame_winds(info, *arrays):
    vmem = pl.BlockSpec(memory_space=pltpu.VMEM)
    return pl.pallas_call(
        frame_kernel,
        out_shape=[
            jax.ShapeDtypeStruct((SIDE, SPAN, WCH), jnp.float32),
            jax.ShapeDtypeStruct((2 * NSLAB, SIDE, SPAN, PART), jnp.float32),
        ],
        in_specs=[pl.BlockSpec(memory_space=pltpu.SMEM)] + [vmem] * 6,
        out_specs=[vmem] * 2,
        compiler_params=pltpu.CompilerParams(vmem_limit_bytes=24 << 20),
        cost_estimate=pl.CostEstimate(flops=16 << 30, bytes_accessed=4 << 20, transcendentals=0),
        name="frame",
    )(info, *arrays)


def window_kernel(
    part, info, wind_ids, cosine,
    before_edge, low, high, after_edge, west, east, wind_ext,
    levels, mix, basis_main, basis_rest, before_0, after_0,
    *others,
):
    before_1, after_1, earlier = others[:3] if part else (None, None, None)
    out, mine, theirs, state_a, state_b, weighted, gram, rest, *spread = others[3 * part :]
    spread = spread[0] if spread else None
    flip, mx, my, mz, mc, turn_west, turn_east = (info[i] for i in range(7))
    lanes = slice(part * 512, part * 512 + PART)
    skip = part * 64

    for r in range(4):
        state_a[4 + r, FIRST : FIRST + COLS] = low[r, :, lanes]
        state_a[8 + r, FIRST : FIRST + COLS] = high[r, :, lanes]
        for row, edge, bulk_0, bulk_1 in (
            (r, before_edge, before_0, before_1),
            (12 + r, after_edge, after_0, after_1),
        ):
            middle = slice(FIRST + 4, FIRST + COLS - 4)
            if part:
                state_a[row, middle, :128] = bulk_0[r, :, 512:]
                state_a[row, middle, 128:] = bulk_1[r]
            else:
                state_a[row, middle] = bulk_0[r]
            for m in range(PART // 128):
                tile = slice(m * 128, (m + 1) * 128)
                where = edge_tile(r, m + part * 4)
                ends = edge[where[0], where[1]]
                state_a[row, FIRST : FIRST + 4, tile] = ends[:4]
                state_a[row, FIRST + COLS - 4 : FIRST + COLS, tile] = ends[4:]
    for r in range(SIDE):
        from_west = jnp.where(turn_west == 0, r, SIDE - 1 - r)
        from_east = jnp.where(turn_east == 0, r, SIDE - 1 - r)
        state_a[1 + r, FIRST - 4 : FIRST] = west[from_west, :, lanes]
        state_a[1 + r, FIRST + COLS : FIRST + COLS + 4] = east[from_east, :, lanes]

    if part:
        spread = wind_ext
    else:
        repeat_winds(wind_ext, levels, lanes, spread)

    up, down = mix[0:1, lanes], mix[1:2, lanes]

    def updated(source, slab, r, c):
        now = source[r, pl.ds(c, 8), :]
        after = source[r + 1, pl.ds(c, 8), :]
        before = source[r - 1, pl.ds(c, 8), :]
        east_side = source[r, pl.ds(c + 1, 8), :]
        west_side = source[r, pl.ds(c - 1, 8), :]
        u = spread[2 * slab, r - 1, pl.ds(c - FIRST + 8, 8), :]
        v = spread[2 * slab + 1, r - 1, pl.ds(c - FIRST + 8, 8), :]
        gain_east = jnp.maximum(u, 0.0) + DIFFUSE
        gain_after = jnp.maximum(v, 0.0) + DIFFUSE
        change = gain_east * (east_side - now) + (gain_east - u) * (west_side - now)
        change += gain_after * (after - now) + (gain_after - v) * (before - now)
        above, below = pltpu.roll(now, PART - 1, 1), pltpu.roll(now, 1, 1)
        change += up * (above - now) - down * (now - below)
        return now + change

    buffers = (state_a, state_b)
    for step in range(STEPS - 1):
        source, target = buffers[step % 2], buffers[(step + 1) % 2]
        slab = wind_ids[step]

        def body(r, carry):
            for c in range(FIRST - 8, FIRST - 8 + SPAN, 8):
                target[r, c : c + 8, :] = updated(source, slab, r, c)
            return carry

        lax.fori_loop(1 + step, EXT - 1 - step, body, 0)

    source = buffers[(STEPS - 1) % 2]
    slab = wind_ids[STEPS - 1]
    own_lanes = lax.broadcasted_iota(jnp.int32, (16, 128), 1) >= skip

    def last(r, carry):
        own = jnp.where(flip == 0, r - D, ROWS - 1 - (r - D))
        share = cosine[own]
        for c in range(0, COLS, 16):
            first = updated(source, slab, r, FIRST + c)
            second = updated(source, slab, r, FIRST + c + 8)
            both = jnp.concatenate([first, second], axis=0)
            if part:
                there = slice(c, c + 16)
                out[own, there, :512] = earlier[own, there, :512]
                out[own, there, 512:640] = jnp.where(
                    own_lanes, both[:, :128], earlier[own, there, 512:]
                )
                out[own, there, 640:] = both[:, 128:]
            else:
                out[own, c : c + 16, :] = both
            weighted[own, c : c + 16, :] = (both * share).astype(jnp.bfloat16)
        return carry

    lax.fori_loop(D, D + ROWS, last, 0)

    flat_weighted = weighted[...].reshape(ROWS * COLS, PART)
    across = (((0,), (0,)), ((), ()))
    for i in range(PART // 128):
        gram[i * 128 : (i + 1) * 128, :] = lax.dot_general(
            flat_weighted[:, i * 128 : (i + 1) * 128],
            basis_main[...],
            across,
            preferred_element_type=jnp.float32,
        )
    tail = lax.dot_general(
        basis_rest[...], flat_weighted, across, preferred_element_type=jnp.float32
    )
    for g in range(8):
        rest[g, :, :LEV] = tail[:, skip + g * LEV : skip + (g + 1) * LEV]

    def place_blocks(i, carry):
        rz, rx, ry = i // 8, (i // 2) % 4, i % 2
        z, x = (mz + rz) % 4, (mx + rx) % 4
        outer, inner = (rx, rz) if part else (rz, rx)
        at = outer * 8 + inner * 2 + ry
        a = x * 2 + (my ^ ry)
        for dc, target in ((0, mine), (1, theirs)):
            g = z * 2 + (mc ^ dc)
            target[at, :LEV] = gram[
                pl.ds(pl.multiple_of(skip + g * LEV, 8), LEV),
                pl.ds(pl.multiple_of(a * 128, 128), 128),
            ]
            target[at, LEV:] = rest[g, pl.ds(pl.multiple_of(a * 16, 16), 16), :]
        return carry

    lax.fori_loop(0, 32, place_blocks, 0, unroll=32)


def window(part, scalars, arrays):
    blocks = jax.ShapeDtypeStruct((32, BLOCK, 128), jnp.float32)
    vmem = pl.BlockSpec(memory_space=pltpu.VMEM)
    return pl.pallas_call(
        functools.partial(window_kernel, part),
        out_shape=[
            jax.ShapeDtypeStruct((ROWS, COLS, CH if part else PART), jnp.float32),
            blocks,
            blocks,
        ],
        in_specs=[pl.BlockSpec(memory_space=pltpu.SMEM)] * len(scalars) + [vmem] * len(arrays),
        out_specs=[vmem] * 3,
        scratch_shapes=[
            pltpu.VMEM((EXT, PITCH, PART), jnp.float32),
            pltpu.VMEM((EXT, PITCH, PART), jnp.float32),
            pltpu.VMEM((ROWS, COLS, PART), jnp.bfloat16),
            pltpu.VMEM((PART, 1024), jnp.float32),
            pltpu.VMEM((8, 128, 128), jnp.float32),
        ]
        + [pltpu.VMEM((2 * NSLAB, SIDE, SPAN, PART), jnp.float32)] * (1 - part),
        compiler_params=pltpu.CompilerParams(vmem_limit_bytes=(24 if part else 32) << 20),
        cost_estimate=pl.CostEstimate(flops=8 << 30, bytes_accessed=16 << 20, transcendentals=0),
        name=f"window_{part}",
    )(*scalars, *arrays)


def line_sum(parts, **axis):
    (name,) = axis
    sent = [lax.ppermute(parts[k], ALL, moved(**{name: k})) for k in (1, 2, 3)]
    return (parts[0] + sent[0]) + (sent[1] + sent[2])


def shards(pool, vec_ids, winds, wind_ids, mixing, basis):
    lat_index = lax.axis_index("lat").astype(jnp.int32)
    lon_index = lax.axis_index("lon").astype(jnp.int32)
    flip = lon_index // 8
    info = jnp.stack(
        [
            flip,
            lat_index // 2,
            lat_index % 2,
            (lon_index // 2) % 4,
            lon_index % 2,
            (lon_index % 8 == 0).astype(jnp.int32),
            (lon_index % 8 == 7).astype(jnp.int32),
        ]
    )
    edge_next, edge_last = lead(info, vec_ids, pool, winds)
    before_edge = lax.ppermute(edge_next, ALL, FORWARD)
    after_edge = lax.ppermute(edge_last, ALL, BACKWARD)
    low, high, wind, next_0, next_1, last_0, last_1, basis_main, basis_rest = pack(
        info, vec_ids, pool, winds, basis
    )
    to_east, to_west, *bulk = edges(
        (before_edge, after_edge, low, high, wind), (next_0, last_0, next_1, last_1)
    )
    west = lax.ppermute(to_east, "lon", EASTWARD)
    east = lax.ppermute(to_west, "lon", WESTWARD)
    before_0, after_0 = lax.ppermute(bulk[0], ALL, FORWARD), lax.ppermute(bulk[1], ALL, BACKWARD)
    before_1, after_1 = lax.ppermute(bulk[2], ALL, FORWARD), lax.ppermute(bulk[3], ALL, BACKWARD)
    levels = jnp.asarray(np.arange(CH, dtype=np.int32)[None] % LEV)
    wind_ext, spread = frame_winds(info, before_edge, after_edge, wind, west, east, levels)

    level_mix = jnp.concatenate(
        [mixing.reshape(TR, LEV - 1), jnp.zeros((TR, 1), mixing.dtype)], axis=1
    )
    upper = jnp.tile(level_mix.reshape(GROUP), VEC)
    mix = jnp.stack([upper, jnp.roll(upper, 1)])
    rows = (jnp.arange(ROWS, dtype=jnp.int32) + lat_index * ROWS).astype(jnp.float32)
    cosine = jnp.cos((rows + 0.5) * (math.pi / (ROWS * 8)) - math.pi / 2)
    scalars = (info, wind_ids, cosine)
    tile = (before_edge, low, high, after_edge, west, east)
    arrays = (levels, mix, basis_main, basis_rest, before_0, after_0)
    half, mine, theirs = window(0, scalars, (*tile, wind_ext, *arrays))
    first = mine + lax.ppermute(theirs, ALL, moved(dc=1))
    sensitivity, mine, theirs = window(
        1, scalars, (*tile, spread, *arrays, before_1, after_1, half)
    )
    second = mine + lax.ppermute(theirs, ALL, moved(dc=1))

    first = line_sum(first.reshape(4, 8, BLOCK, 128), dz=1)
    second = line_sum(second.reshape(4, 8, BLOCK, 128), dx=1)
    first = line_sum(first.reshape(4, 2, BLOCK, 128), dx=1)
    second = line_sum(second.reshape(4, 2, BLOCK, 128), dz=1)
    near = jnp.where(flip == 0, first, second)
    far = jnp.where(flip == 0, second, first)
    block = near[0] + lax.ppermute(near[1], ALL, turned(1))
    block += lax.ppermute(far[0], ALL, turned(2)) + lax.ppermute(far[1], ALL, turned(3))
    ritz = jnp.concatenate([block[:LEV].T, block[LEV:, :LEV]], axis=0)
    return sensitivity, ritz * (1.0 / math.sqrt(ROWS * COLS * 128))


def solution(mesh):
    in_specs = (P("lat", "lon", None), P(), P("lat", "lon", None), P(), P(), P("lat", "lon", None))
    out_specs = (P("lat", "lon", None), P("lat", "lon"))
    return jax.shard_map(shards, mesh=mesh, in_specs=in_specs, out_specs=out_specs, check_vma=False)
```
